32 devices in a mesh: crop: 2 (over y), space: 16 (over z, x, core).
Axes of the slice: x: 2, y: 2, z: 4, core: 2. Of those that a mesh axis runs over, the one named last changes fastest.
Arguments:
- features: bfloat16 [128, 8, 8, 192], P(('crop', 'space')), parts along dimension 0, may hold values from -6 to 6
- cotangent: bfloat16 [128, 8, 8, 192], P(('crop', 'space')), parts along dimension 0, may hold values from -6 to 6
- kernel: float32 [7, 7, 7, 192], replicated, may hold values from -0.3125 to 0.3125
- b_dw: float32 [192], replicated, may hold values from -3 to 3
- ln_gain: float32 [192], replicated, may hold values from 0.5 to 1.5
- ln_bias: float32 [192], replicated, may hold values from -3 to 3
- w_in_t: bfloat16 [768, 192], P('space'), may hold values from -0.4375 to 0.4375
- b_in: bfloat16 [768], P('space'), may hold values from -3 to 3
- w_out: bfloat16 [768, 192], P('space'), may hold values from -0.21875 to 0.21875
- b_out: float32 [192], replicated, may hold values from -3 to 3
- gamma: float32 [192], replicated, may hold values from 0.5 to 1.5
Outputs:
- block_out: bfloat16 [128, 8, 8, 192], P(('crop', 'space')), parts along dimension 0
- d_x: bfloat16 [128, 8, 8, 192], P(('crop', 'space')), parts along dimension 0
- d_kernel: float32 [14, 7, 7, 192], P('crop'), parts along dimension 0
- d_b_dw: float32 [384], P('crop'), parts along dimension 0
- d_ln_gain: float32 [384], P('crop'), parts along dimension 0
- d_ln_bias: float32 [384], P('crop'), parts along dimension 0
- d_w_in: float32 [1536, 192], P(('crop', 'space')), parts along dimension 0
- d_b_in: float32 [1536], P(('crop', 'space')), parts along dimension 0
- d_w_out: float32 [1536, 192], P(('crop', 'space')), parts along dimension 0
- d_b_out: float32 [384], P('crop'), parts along dimension 0
- d_gamma: float32 [384], P('crop'), parts along dimension 0
The draws below stay inside these ranges and needn't reach their ends.
There are 2 independent parts, one for each index of `crop`. The reference program is written for one: setup_inputs(seed, part) draws one part's arguments, and reference() takes and returns one part's arrays. A program takes and returns all parts, laid end to end along the dimension named above; an argument that names none is the same for every part. Nothing has to cross between parts.
All inputs are finite; a program needn't handle non-finite values.
Results may differ from the reference program's by a relative error of at most 0.0065.
Values may be sent and summed in bfloat16 or wider, within the bound.
No kernel may reach another device: no remote copies, remote signals or barrier semaphores. Data moves between devices by JAX's collectives and lax.ppermute only.
A program may use at most 64 MiB of HBM per device.

```python
import jax
import jax.numpy as jnp
from jax import lax

C = 192
H = 768
KS = 7
SLAB = 4
GY = 8
GZ = 8
GX = 64


def shard_levels(own_key, shape, split, least, largest):
    level, own = 1.0, jax.random.fold_in(own_key, 6)
    for position, parts in split:
        draws = jnp.exp(jax.random.uniform(jax.random.fold_in(own, position), (parts,), jnp.float32, least / len(split), largest / len(split)))
        level = level * jnp.repeat(draws, shape[position] // parts).reshape([-1 if axis == position else 1 for axis in range(len(shape))])
    return level


def noise(rng, extent, deviation, most, pieces=(), held_as=jnp.bfloat16):
    array = jax.random.normal(rng, extent, jnp.float32) * deviation
    if len(pieces) > 0:
        array = shard_levels(rng, extent, pieces, -0.22, 0.18) * array
    return jnp.clip(array, min=-most, max=most).astype(held_as)


def setup_inputs(seed: int = 0, part: int = 0) -> dict:
    key_list = jax.random.split(jax.random.key(seed), 12)
    part_splits = jax.random.split(jax.random.fold_in(key_list[11], part), 12)
    features = noise(part_splits[0], (GX, GY, GZ, C), 1.0, 6.0, ((0, 16),))
    cotangent = noise(part_splits[1], (GX, GY, GZ, C), 1.0, 6.0, ((0, 16),))
    kernel = noise(key_list[2], (KS, KS, KS, C), (KS * KS * KS) ** -0.5, 0.3125, (), jnp.float32)
    b_dw = noise(key_list[3], (C,), 0.5, 3.0, (), jnp.float32)
    ln_gain = jnp.clip(jax.random.uniform(key_list[4], (C,), jnp.float32, 0.5, 1.5), 0.5, 1.5)
    ln_bias = noise(key_list[5], (C,), 0.5, 3.0, (), jnp.float32)
    w_in_t = noise(key_list[6], (H, C), C ** -0.5, 0.4375, ((0, 16),))
    b_in = noise(key_list[7], (H,), 0.5, 3.0, ((0, 16),))
    w_out = noise(key_list[8], (H, C), H ** -0.5, 0.21875, ((0, 16),))
    b_out = noise(key_list[9], (C,), 0.5, 3.0, (), jnp.float32)
    gamma = jnp.clip(jax.random.uniform(key_list[10], (C,), jnp.float32, 0.5, 1.5), 0.5, 1.5)
    return {"features": features, "cotangent": cotangent, "kernel": kernel, "b_dw": b_dw, "ln_gain": ln_gain, "ln_bias": ln_bias, "w_in_t": w_in_t, "b_in": b_in, "w_out": w_out, "b_out": b_out, "gamma": gamma}


root_half = 0.7071067811865476
inv_root_tau = 0.3989422804014327

def gelu_value(pre):
    return 0.5 * pre * (1.0 + lax.erf(pre * root_half))

def gelu_slope(pre):
    return 0.5 * (1.0 + lax.erf(pre * root_half)) + pre * jnp.exp(-0.5 * pre * pre) * inv_root_tau

def stencil(padded, kernel, size_x, size_y, size_z):
    width = kernel.shape[0]
    total = jnp.zeros((size_x, size_y, size_z, padded.shape[3]), jnp.float32)
    for along_x in range(width):
        for along_y in range(width):
            for along_z in range(width):
                window = padded[along_x:along_x + size_x, along_y:along_y + size_y, along_z:along_z + size_z]
                total = total + window.astype(jnp.float32) * kernel[along_x, along_y, along_z]
    return total

def kernel_terms(padded, grad, width):
    size_x, size_y, size_z, chans = grad.shape
    grad_f = grad.astype(jnp.float32)
    terms = []
    for along_x in range(width):
        for along_y in range(width):
            for along_z in range(width):
                window = padded[along_x:along_x + size_x, along_y:along_y + size_y, along_z:along_z + size_z]
                terms.append(lax.optimization_barrier(jnp.sum(window.astype(jnp.float32) * grad_f, axis=(0, 1, 2))))
    return jnp.stack(terms).reshape(width, width, width, chans)

def reference(features, cotangent, kernel, b_dw, ln_gain, ln_bias, w_in_t, b_in, w_out, b_out, gamma):
    size_x, size_y, size_z, chans = features.shape
    width = kernel.shape[0]
    half = width // 2
    scale = float(size_x * size_y * size_z) ** (-0.5)
    padded = jnp.pad(features, ((half, half), (half, half), (half, half), (0, 0)))
    mixed = stencil(padded, kernel, size_x, size_y, size_z) + b_dw
    centred = mixed - lax.optimization_barrier(jnp.mean(mixed, axis=-1, keepdims=True))
    inverse = lax.rsqrt(lax.optimization_barrier(jnp.mean(centred * centred, axis=-1, keepdims=True)) + 1e-06)
    unit_value = centred * inverse
    normed = (unit_value * ln_gain + ln_bias).astype(jnp.bfloat16)
    block_rows = SLAB * GY * GZ
    blocks = size_x * size_y * size_z // block_rows
    normed_b = normed.reshape(blocks, block_rows, chans)
    input_b = features.reshape(blocks, block_rows, chans)
    cot_b = cotangent.reshape(blocks, block_rows, chans)
    hidden_units = w_in_t.shape[0]
    b_in_f = b_in.astype(jnp.float32)

    def one_block(carry, items):
        acc_wi, acc_bi, acc_wo, acc_bo, acc_gm = carry
        normed_rows, input_rows, cot_rows = items
        pre = lax.dot_general(normed_rows, w_in_t, (((1,), (1,)), ((), ())), preferred_element_type=jnp.float32) + b_in_f
        hidden = gelu_value(pre).astype(jnp.bfloat16)
        branch = jnp.dot(hidden, w_out, preferred_element_type=jnp.float32) + b_out
        output = (input_rows.astype(jnp.float32) + gamma * branch).astype(jnp.bfloat16)
        cot_f = cot_rows.astype(jnp.float32)
        d_branch = gamma * cot_f
        d_branch_b = d_branch.astype(jnp.bfloat16)
        d_hidden = lax.dot_general(d_branch_b, w_out, (((1,), (1,)), ((), ())), preferred_element_type=jnp.float32)
        d_pre = d_hidden * gelu_slope(pre)
        d_pre_b = d_pre.astype(jnp.bfloat16)
        d_normed = jnp.dot(d_pre_b, w_in_t, preferred_element_type=jnp.float32)
        acc_wo = acc_wo + lax.dot_general(hidden, d_branch_b, (((0,), (0,)), ((), ())), preferred_element_type=jnp.float32)
        acc_wi = acc_wi + lax.dot_general(d_pre_b, normed_rows, (((0,), (0,)), ((), ())), preferred_element_type=jnp.float32)
        acc_bi = acc_bi + lax.optimization_barrier(jnp.sum(d_pre, axis=0))
        acc_bo = acc_bo + lax.optimization_barrier(jnp.sum(d_branch, axis=0))
        acc_gm = acc_gm + lax.optimization_barrier(jnp.sum(cot_f * branch, axis=0))
        return ((acc_wi, acc_bi, acc_wo, acc_bo, acc_gm), (output, d_normed))
    start = (jnp.zeros((hidden_units, chans), jnp.float32), jnp.zeros((hidden_units,), jnp.float32), jnp.zeros((hidden_units, chans), jnp.float32), jnp.zeros((chans,), jnp.float32), jnp.zeros((chans,), jnp.float32))
    sums, outs = lax.scan(one_block, start, (normed_b, input_b, cot_b))
    acc_wi, acc_bi, acc_wo, acc_bo, acc_gm = sums
    output = outs[0].reshape(size_x, size_y, size_z, chans)
    d_normed = outs[1].reshape(size_x, size_y, size_z, chans)
    d_ln_gain = lax.optimization_barrier(jnp.sum(d_normed * unit_value, axis=(0, 1, 2)))
    d_ln_bias = lax.optimization_barrier(jnp.sum(d_normed, axis=(0, 1, 2)))
    scaled = d_normed * ln_gain
    d_mixed = inverse * (scaled - lax.optimization_barrier(jnp.mean(scaled, axis=-1, keepdims=True)) - unit_value * lax.optimization_barrier(jnp.mean(scaled * unit_value, axis=-1, keepdims=True)))
    d_b_dw = lax.optimization_barrier(jnp.sum(d_mixed, axis=(0, 1, 2)))
    d_mixed_b = d_mixed.astype(jnp.bfloat16)
    d_kernel = kernel_terms(padded, d_mixed_b, width)
    grad_pad = jnp.pad(d_mixed_b, ((half, half), (half, half), (half, half), (0, 0)))
    back = stencil(grad_pad, kernel[::-1, ::-1, ::-1], size_x, size_y, size_z)
    d_x = (cotangent.astype(jnp.float32) + back).astype(jnp.bfloat16)
    return (output, d_x, d_kernel * scale, d_b_dw * scale, d_ln_gain * scale, d_ln_bias * scale, acc_wi * scale, acc_bi * scale, acc_wo * scale, acc_bo * scale, acc_gm * scale)
```

```python
import jax
import jax.numpy as jnp
from jax import lax
from jax.experimental import pallas as pl
from jax.experimental.pallas import tpu as pltpu
from jax.sharding import PartitionSpec as P

root_half = 0.7071067811865476
inv_root_tau = 0.3989422804014327
F32 = jnp.float32
BF16 = jnp.bfloat16
LANE = 128
VMEM = pl.BlockSpec(memory_space=pltpu.VMEM)
SMEM = pl.BlockSpec(memory_space=pltpu.SMEM)


def swap(x, bit):
    size = lax.axis_size("space")
    return lax.ppermute(x, "space", [(i, i ^ bit) for i in range(size)])


def swap_odd(x):
    size = lax.axis_size("space")
    pairs = [(i, i + 1) for i in range(1, size - 1, 2)]
    return lax.ppermute(x, "space", pairs + [(j, i) for i, j in pairs])


def shifted(v, by):
    if by == 0:
        return v
    row = lax.broadcasted_iota(jnp.int32, v.shape, 0)
    keep = (row < 8 - by) if by > 0 else (row >= -by)
    return jnp.where(keep, pltpu.roll(v, (-by) % 8, axis=0), 0.0)


def fill_planes(odd, x_ref, p_ref, q_ref, z_ref):
    for plane in range(10):
        if plane < 3:
            v = jnp.where(odd, p_ref[plane + 1].astype(F32), q_ref[plane + 1].astype(F32))
        elif plane < 7:
            v = x_ref[plane - 3].astype(F32)
        else:
            v = jnp.where(odd, q_ref[plane - 7].astype(F32), p_ref[plane - 7].astype(F32))
        z_ref[plane] = v[:, :, :LANE]
        rest = v[:, :, LANE:]
        if plane < 8:
            z_ref[10 + plane, :, :, 0:64] = rest
        if plane >= 2:
            z_ref[8 + plane, :, :, 64:128] = rest


def fill_taps(k_ref, t_ref):
    for a in range(7):
        for b in range(7):
            v = k_ref[a, b]
            t_ref[0, a, b, 0:7] = v[:, :LANE]
            t_ref[1, a, b, 0:7, 0:64] = v[:, LANE:]
            t_ref[1, a, b, 0:7, 64:128] = v[:, LANE:]


def stencil(z_ref, t_ref, u_ref, flip):
    def unit(u, carry):
        base = jnp.where(u < 4, u, u + 6)
        group = jnp.where(u < 4, 0, 1)
        total = [None] * 8
        for e in range(7):
            acc = [None] * 8
            for a in range(7):
                taps = []
                for b in range(7):
                    fa, fb, fe = (6 - a, 6 - b, 6 - e) if flip else (a, b, e)
                    taps.append(jnp.broadcast_to(t_ref[group, fa, fb, fe : fe + 1], (8, LANE)))
                for source in range(8):
                    x = z_ref[base + a, source]
                    for b in range(7):
                        j = source - b + 3
                        if 0 <= j < 8:
                            term = x * taps[b]
                            acc[j] = term if acc[j] is None else acc[j] + term
            for j in range(8):
                part = shifted(acc[j], e - 3)
                total[j] = part if total[j] is None else total[j] + part
        for j in range(8):
            u_ref[u, j] = total[j]
        return carry

    lax.fori_loop(0, 6, unit, 0)


def forward_kernel(odd_ref, x_ref, p_ref, q_ref, k_ref, vec_ref, na_ref, unit_ref, z_ref, t_ref, u_ref, m_ref):
    fill_planes(odd_ref[0] == 1, x_ref, p_ref, q_ref, z_ref)
    fill_taps(k_ref, t_ref)
    stencil(z_ref, t_ref, u_ref, False)
    for i in range(4):
        m_ref[64 * i : 64 * i + 64, 0:LANE] = u_ref[i].reshape(64, LANE)
    for i in range(2):
        v = u_ref[4 + i].reshape(64, LANE)
        m_ref[64 * i : 64 * i + 64, LANE : LANE + 64] = v[:, 0:64]
        m_ref[64 * i + 128 : 64 * i + 192, LANE : LANE + 64] = v[:, 64:128]
    chans = k_ref.shape[3]
    mixed = m_ref[...] + vec_ref[0:1]
    centred = mixed - jnp.mean(mixed, axis=-1, keepdims=True)
    inverse = lax.rsqrt(jnp.mean(centred * centred, axis=-1, keepdims=True) + 1e-06)
    unit = centred * inverse
    normed = unit * vec_ref[1:2] + vec_ref[2:3]
    rows = unit.shape[0]
    na_ref[:, 0:chans] = normed.astype(BF16)
    one = (lax.broadcasted_iota(jnp.int32, (rows, 256 - chans), 1) == 0).astype(F32)
    na_ref[:, chans:256] = one.astype(BF16)
    unit_ref[:, 0:chans] = unit
    unit_ref[:, chans:256] = jnp.broadcast_to(inverse, (rows, 256 - chans))


def pointwise_kernel(g0_ref, g1_ref, na_ref, unit_ref, x_ref, c_ref, vec_ref, out_ref, dm_ref, w0_ref, w1_ref, small_ref):
    rows, chans = na_ref.shape[0], x_ref.shape[3]
    normed = na_ref[...]
    cot = c_ref[...].astype(F32).reshape(rows, chans)
    gamma = vec_ref[4:5]
    d_branch = cot * gamma
    d_b = jnp.concatenate([d_branch, jnp.zeros((rows, 256 - chans), F32)], axis=1).astype(BF16)
    branch = jnp.zeros((rows, 256), F32)
    d_normed = jnp.zeros((rows, 256), F32)
    over_c = (((1,), (1,)), ((), ()))
    over_rows = (((0,), (0,)), ((), ()))
    for g_ref, w_ref in ((g0_ref, w0_ref), (g1_ref, w1_ref)):
        step = 128
        for first in range(0, g_ref.shape[0], step):
            here = slice(first, first + step)
            w_in = g_ref[here, 0:256]
            w_out = g_ref[here, 256:512]
            pre = lax.dot_general(normed, w_in, over_c, preferred_element_type=F32)
            d_hidden = lax.dot_general(d_b, w_out, over_c, preferred_element_type=F32)
            cdf = 0.5 * (1.0 + lax.erf(pre * root_half))
            hidden = (pre * cdf).astype(BF16)
            slope = cdf + pre * jnp.exp(-0.5 * pre * pre) * inv_root_tau
            d_pre = (d_hidden * slope).astype(BF16)
            branch = branch + jnp.dot(hidden, w_out, preferred_element_type=F32)
            d_normed = d_normed + jnp.dot(d_pre, w_in, preferred_element_type=F32)
            w_ref[here, 0:256] = lax.dot_general(d_pre, normed, over_rows, preferred_element_type=F32).astype(BF16)
            w_ref[here, 256:512] = lax.dot_general(hidden, d_b, over_rows, preferred_element_type=F32).astype(BF16)
    branch = branch[:, 0:chans] + vec_ref[3:4]
    x = x_ref[...].astype(F32).reshape(rows, chans)
    out_ref[...] = (x + gamma * branch).reshape(out_ref.shape).astype(BF16)
    d_normed = d_normed[:, 0:chans]
    unit = unit_ref[:, 0:chans]
    inverse = unit_ref[:, chans : chans + 1]
    scaled = d_normed * vec_ref[1:2]
    d_mixed = inverse * (
        scaled
        - jnp.mean(scaled, axis=-1, keepdims=True)
        - unit * jnp.mean(scaled * unit, axis=-1, keepdims=True)
    )
    dm_ref[...] = d_mixed.reshape(dm_ref.shape).astype(BF16)
    small_ref[...] = jnp.zeros(small_ref.shape, F32)
    sums = (d_mixed, d_normed * unit, d_normed, d_branch, cot * branch)
    for i, term in enumerate(sums):
        small_ref[i : i + 1, 0:chans] = jnp.sum(term, axis=0, keepdims=True)


def rows_to_one(v):
    row = lax.broadcasted_iota(jnp.int32, (8, LANE), 0)
    v = list(v) + [jnp.zeros((8, LANE), F32)]
    for half in (4, 2, 1):
        low = (row & half) == 0
        v = [
            jnp.where(low, v[i], v[i + half])
            + jnp.where(
                low,
                pltpu.roll(v[i], 8 - half, axis=0),
                pltpu.roll(v[i + half], half, axis=0),
            )
            for i in range(half)
        ]
    return v[0]


HALF = 320


def grad_kernel(odd_ref, x_ref, p_ref, q_ref, g_ref, small_ref, keep_ref, send_ref, z_ref, s_ref, wa_ref, wb_ref, w_ref):
    odd = odd_ref[0]
    fill_planes(odd == 1, x_ref, p_ref, q_ref, z_ref)
    for i in range(4):
        v = g_ref[i].astype(F32)
        s_ref[3, i] = v[:, :, :LANE]
        s_ref[3, 4 + i % 2, :, :, 64 * (i // 2) : 64 * (i // 2) + 64] = v[:, :, LANE:]

    def shift_unit(u, carry):
        for j in range(8):
            v = s_ref[3, u, j]
            for e in range(7):
                if e != 3:
                    s_ref[e, u, j] = shifted(v, 3 - e)
        return carry

    lax.fori_loop(0, 6, shift_unit, 0)

    def over_a(a, carry):
        for e in range(7):
            for units, into in (((0, 1, 2, 3), wa_ref), ((4, 5), wb_ref)):
                acc = [None] * 7
                for u in units:
                    base = u if u < 4 else u + 6
                    grads = [s_ref[e, u, j] for j in range(8)]
                    for source in range(8):
                        x = z_ref[base + a, source]
                        for b in range(7):
                            j = source - b + 3
                            if 0 <= j < 8:
                                term = x * grads[j]
                                acc[b] = term if acc[b] is None else acc[b] + term
                one = rows_to_one(acc)
                if len(units) == 2:
                    one = one + pltpu.roll(one, 64, axis=1)
                into[pl.ds(a * 64 + e, 8, stride=8), :] = one
        return carry

    for b in range(49):
        at = 64 * (b // 7) + 8 * (b % 7)
        wa_ref[at : at + 8] = jnp.zeros((8, LANE), F32)
        wb_ref[at : at + 8] = jnp.zeros((8, LANE), F32)
    lax.fori_loop(0, 7, over_a, 0)

    low = lax.broadcasted_iota(jnp.int32, (56, LANE), 1) < 64
    for a in range(5):
        w_ref[0, 56 * a : 56 * a + 56] = wa_ref[64 * a : 64 * a + 56]
    w_ref[0, 280:288] = small_ref[:, 0:LANE]
    w_ref[0, 288:HALF] = jnp.zeros((HALF - 288, LANE), F32)
    for a in range(5, 7):
        w_ref[1, 56 * (a - 5) : 56 * (a - 5) + 56] = wa_ref[64 * a : 64 * a + 56]
    for a in range(3):
        w_ref[1, 112 + 56 * a : 168 + 56 * a] = jnp.where(
            low, wb_ref[64 * a : 64 * a + 56], wb_ref[64 * (a + 4) : 64 * (a + 4) + 56]
        )
    w_ref[1, 280:312] = jnp.where(low[0:32], wb_ref[192:224], wb_ref[224:256])
    w_ref[1, 312:320] = small_ref[:, LANE:256]
    keep_ref[...] = w_ref[odd].astype(BF16)
    send_ref[...] = w_ref[1 - odd].astype(BF16)


def unpack_kernel(scale, odd_ref, mine_ref, other_ref, dk_ref, small_ref, w_ref):
    odd = odd_ref[0]
    w_ref[odd] = mine_ref[...].astype(F32) * scale
    w_ref[1 - odd] = other_ref[...].astype(F32) * scale
    for a in range(7):
        for b in range(7):
            row = 56 * a + 8 * b if a < 5 else 56 * (a - 5) + 8 * b
            main = w_ref[0 if a < 5 else 1, row : row + 7]
            if a == 3:
                at, lane = 280 + 8 * (b % 4), 64 * (b // 4)
            else:
                at, lane = 112 + 56 * (a % 4) + 8 * b, 64 * (a // 4)
            rest = w_ref[1, at : at + 7]
            dk_ref[a, b, :, 0:LANE] = main
            dk_ref[a, b, :, LANE : LANE + 64] = rest[:, lane : lane + 64]
    small_ref[:, 0:LANE] = w_ref[0, 280:288]
    small_ref[:, LANE:256] = w_ref[1, 312:320]


def back_kernel(odd_ref, g_ref, p_ref, q_ref, k_ref, c_ref, dx_ref, z_ref, t_ref, u_ref):
    fill_planes(odd_ref[0] == 1, g_ref, p_ref, q_ref, z_ref)
    fill_taps(k_ref, t_ref)
    stencil(z_ref, t_ref, u_ref, True)
    for i in range(4):
        cot = c_ref[i].astype(F32)
        dx_ref[i, :, :, 0:LANE] = (cot[:, :, 0:LANE] + u_ref[i]).astype(BF16)
        v = u_ref[4 + i % 2]
        rest = v[:, :, 64 * (i // 2) : 64 * (i // 2) + 64]
        dx_ref[i, :, :, LANE : LANE + 64] = (cot[:, :, LANE:] + rest).astype(BF16)


def params(mib):
    return pltpu.CompilerParams(vmem_limit_bytes=mib * 1024 * 1024)


def struct(shape, dtype):
    return jax.ShapeDtypeStruct(shape, dtype)


def on_device(
    features, cotangent, kernel, b_dw, ln_gain, ln_bias, w_in_t, b_in, w_out, b_out, gamma
):
    size_x, size_y, size_z, chans = features.shape
    devices = lax.axis_size("space")
    scale = float(size_x * devices * size_y * size_z) ** (-0.5)
    rows = size_x * size_y * size_z
    units = w_in_t.shape[0]
    bits = [1 << i for i in range(devices.bit_length() - 1)]
    odd = lax.rem(lax.axis_index("space"), 2).astype(jnp.int32).reshape(1)
    vecs = jnp.stack([b_dw, ln_gain, ln_bias, b_out, gamma, gamma, gamma, gamma])

    weights = jnp.concatenate(
        [
            w_in_t,
            b_in[:, None],
            jnp.zeros((units, 255 - chans), BF16),
            w_out,
            jnp.zeros((units, 256 - chans), BF16),
        ],
        axis=1,
    )
    for bit in bits[:0:-1]:
        weights = jnp.concatenate([weights, swap(weights, bit)], axis=0)
    weights_other = swap(weights, 1)
    x_core, x_far = swap(features, 1), swap_odd(features)

    z_scratch = pltpu.VMEM((18, size_y, size_z, LANE), F32)
    t_scratch = pltpu.VMEM((2, 7, 7, 8, LANE), F32)
    u_scratch = pltpu.VMEM((6, size_y, size_z, LANE), F32)
    normed, unit = pl.pallas_call(
        forward_kernel,
        out_shape=(struct((rows, 256), BF16), struct((rows, 256), F32)),
        in_specs=[SMEM] + [VMEM] * 5,
        out_specs=(VMEM, VMEM),
        scratch_shapes=[z_scratch, t_scratch, u_scratch, pltpu.VMEM((rows, chans), F32)],
        compiler_params=params(12),
        name="forward_stencil",
    )(odd, features, x_core, x_far, kernel, vecs)

    half = weights.shape[0]
    output, d_mixed, grad_keep, grad_send, small = pl.pallas_call(
        pointwise_kernel,
        out_shape=(
            struct(features.shape, BF16),
            struct(features.shape, BF16),
            struct((half, 512), BF16),
            struct((half, 512), BF16),
            struct((8, 256), F32),
        ),
        in_specs=[VMEM] * 7,
        out_specs=(VMEM,) * 5,
        compiler_params=params(16),
        name="pointwise",
    )(weights, weights_other, normed, unit, features, cotangent, vecs)

    g_core, g_far = swap(d_mixed, 1), swap_odd(d_mixed)

    total = grad_keep.astype(F32) + swap(grad_send, 1).astype(F32)
    for bit in bits[1:]:
        n = total.shape[0] // 2
        sent = total[n:].astype(BF16)
        total = total[:n] + swap(sent, bit).astype(F32)
    total = total * scale
    d_w_in, d_b_in, d_w_out = (
        total[:, 0:chans],
        total[:, chans],
        total[:, 256 : 256 + chans],
    )

    keep, send = pl.pallas_call(
        grad_kernel,
        out_shape=(struct((HALF, LANE), BF16), struct((HALF, LANE), BF16)),
        in_specs=[SMEM] + [VMEM] * 5,
        out_specs=(VMEM, VMEM),
        scratch_shapes=[
            z_scratch,
            pltpu.VMEM((7, 6, size_y, size_z, LANE), F32),
            pltpu.VMEM((448, LANE), F32),
            pltpu.VMEM((448, LANE), F32),
            pltpu.VMEM((2, HALF, LANE), F32),
        ],
        compiler_params=params(12),
        name="kernel_gradient",
    )(odd, features, x_core, x_far, d_mixed, small)
    mine = keep.astype(F32) + swap(send, 1).astype(F32)
    for bit in bits[1:]:
        sent = mine.astype(BF16)
        mine = sent.astype(F32) + swap(sent, bit).astype(F32)
    mine = mine.astype(BF16)
    other = swap(mine, 1)

    d_x = pl.pallas_call(
        back_kernel,
        out_shape=struct(features.shape, BF16),
        in_specs=[SMEM] + [VMEM] * 5,
        out_specs=VMEM,
        scratch_shapes=[z_scratch, t_scratch, u_scratch],
        compiler_params=params(12),
        name="backward_stencil",
    )(odd, d_mixed, g_core, g_far, kernel, cotangent)

    d_kernel, sums = pl.pallas_call(
        lambda *refs: unpack_kernel(scale, *refs),
        out_shape=(struct(kernel.shape, F32), struct((8, 256), F32)),
        in_specs=[SMEM] + [VMEM] * 2,
        out_specs=(VMEM, VMEM),
        scratch_shapes=[pltpu.VMEM((2, HALF, LANE), F32)],
        compiler_params=params(4),
        name="unpack",
    )(odd, mine, other)
    return (
        output,
        d_x,
        d_kernel,
        sums[0, :chans],
        sums[1, :chans],
        sums[2, :chans],
        d_w_in,
        d_b_in,
        d_w_out,
        sums[3, :chans],
        sums[4, :chans],
    )


def solution(mesh):
    in_specs = (
        P(("crop", "space"), None, None, None),
        P(("crop", "space"), None, None, None),
        P(),
        P(),
        P(),
        P(),
        P("space", None),
        P("space"),
        P("space", None),
        P(),
        P(),
    )
    out_specs = (
        P(("crop", "space"), None, None, None),
        P(("crop", "space"), None, None, None),
        P("crop", None, None, None),
        P("crop"),
        P("crop"),
        P("crop"),
        P(("crop", "space"), None),
        P(("crop", "space")),
        P(("crop", "space"), None),
        P("crop"),
        P("crop"),
    )
    return jax.shard_map(
        on_device, mesh=mesh, in_specs=in_specs, out_specs=out_specs, check_vma=False
    )
```

```python
import functools

import jax
import jax.numpy as jnp
import numpy as np
from jax import lax
from jax.experimental import pallas as pl
from jax.experimental.pallas import tpu as pltpu
from jax.sharding import PartitionSpec as P

root_half = 0.7071067811865476
inv_root_tau = 0.3989422804014327
F32 = jnp.float32
BF16 = jnp.bfloat16
LANE = 128
VMEM = pl.BlockSpec(memory_space=pltpu.VMEM)
HBM = pl.BlockSpec(memory_space=pltpu.HBM)
SMEM = pl.BlockSpec(memory_space=pltpu.SMEM)

POINTS = (0.4, 0.8, 1.25, 2.5)
PAIRS = len(POINTS)


def analysis():
    finite = [0.0] + [sign * p for p in POINTS for sign in (1.0, -1.0)]
    vander = np.array([[x**k for k in range(10)] for x in finite] + [[0.0] * 9 + [1.0]])
    inverse = np.linalg.inv(vander).T
    even = [{k: float(inverse[1 + 2 * q, k]) for k in (2, 4, 6, 8)} for q in range(PAIRS)]
    odd = [{k: float(inverse[1 + 2 * q, k]) for k in (1, 3, 5, 7)} for q in range(PAIRS)]
    zero = {k: float(inverse[0, k]) for k in (0, 2, 4, 6, 8)}
    infinity = {k: float(inverse[9, k]) for k in (1, 3, 5, 7, 9)}
    return even, odd, zero, infinity


def evaluation(size):
    even = [{k: p**k for k in range(0, size, 2)} for p in POINTS]
    odd = [{k: p**k for k in range(1, size, 2)} for p in POINTS]
    return even, odd, {0: 1.0}, {size - 1: 1.0}


def weighted(load, weights):
    total = None
    for k, w in weights.items():
        term = load(k) if w == 1.0 else load(k) * w
        total = term if total is None else total + term
    return total


def low_lanes(shape):
    return lax.broadcasted_iota(jnp.int32, shape, len(shape) - 1) < 64


def to_points(tables, main, rest, store):
    even, odd, zero, infinity = tables
    for q in range(PAIRS):
        e, o = weighted(main, even[q]), weighted(main, odd[q])
        store(1 + 2 * q, e + o)
        store(2 + 2 * q, e - o)
        e, o = weighted(rest, even[q]), weighted(rest, odd[q])
        store(10 + q, jnp.where(low_lanes(e.shape), e + o, e - o))
    store(0, weighted(main, zero))
    store(9, weighted(main, infinity))
    z, i = weighted(rest, zero), weighted(rest, infinity)
    store(14, jnp.where(low_lanes(z.shape), z, i))


def from_points(size, load, power=0):
    main, rest = [None] * size, [None] * size

    def add(into, k, v, w):
        term = v if w == 1.0 else v * w
        into[k] = term if into[k] is None else into[k] + term

    for q in range(PAIRS):
        plus, minus, both = load(1 + 2 * q), load(2 + 2 * q), load(10 + q)
        swapped = pltpu.roll(both, 64, axis=both.ndim - 1)
        sums = (plus + minus, both + swapped), (plus - minus, both - swapped)
        for k in range(size):
            m, r = sums[k % 2]
            add(main, k, m, POINTS[q] ** (k + power))
            add(rest, k, r, POINTS[q] ** (k + power))
    ends = load(14)
    add(main, 0, load(0), 1.0)
    add(rest, 0, ends, 1.0)
    add(main, size - 1, load(9), 1.0)
    add(rest, size - 1, pltpu.roll(ends, 64, axis=ends.ndim - 1), 1.0)
    return main, rest


def swap(x, bit):
    size = lax.axis_size("space")
    return lax.ppermute(x, "space", [(i, i ^ bit) for i in range(size)])


def swap_odd(x):
    size = lax.axis_size("space")
    return lax.ppermute(x, "space", [(i, (i + 1 if i % 2 else i - 1) % size) for i in range(size)])


def shifted(v, by):
    if by == 0:
        return v
    row = lax.broadcasted_iota(jnp.int32, v.shape, 0)
    keep = (row < 8 - by) if by > 0 else (row >= -by)
    return jnp.where(keep, pltpu.roll(v, (-by) % 8, axis=0), 0.0)


def split(v, z_ref, plane):
    z_ref[0, plane] = v[..., :LANE]
    z_ref[1, plane, ..., 0:64] = v[..., LANE:]
    z_ref[1, plane, ..., 64:128] = v[..., LANE:]


def pack_planes(first, load, out_ref):
    for k in range(3):
        v = load(first + k)
        cells = v.shape[0]
        at = k * cells * 3 // 2
        out_ref[at : at + cells] = v[:, :LANE].astype(BF16)
        pair = jnp.concatenate([v[: cells // 2, LANE:], v[cells // 2 :, LANE:]], axis=1)
        out_ref[at + cells : at + cells * 3 // 2] = pair.astype(BF16)


def fill_rim(last, me_ref, p_ref, q_ref, z_ref):
    me = me_ref[0]
    odd = lax.rem(me, 2) == 1
    p, q = p_ref[...].astype(F32), q_ref[...].astype(F32)
    before = jnp.where(me == 0, 0.0, jnp.where(odd, p, q))
    after = jnp.where(me == last, 0.0, jnp.where(odd, q, p))
    rows, cols = z_ref.shape[2], z_ref.shape[3]
    cells = rows * cols
    for k in range(3):
        at = k * cells * 3 // 2
        for v, plane in ((before, k), (after, k + 7)):
            z_ref[0, plane] = v[at : at + cells].reshape(rows, cols, LANE)
            pair = v[at + cells : at + cells * 3 // 2]
            swapped = pltpu.roll(pair, 64, axis=1)
            low = low_lanes(pair.shape)
            z_ref[1, plane, : rows // 2] = jnp.where(low, pair, swapped).reshape(rows // 2, cols, LANE)
            z_ref[1, plane, rows // 2 :] = jnp.where(low, swapped, pair).reshape(rows // 2, cols, LANE)


def fill_taps(k_ref, r_ref, t_ref):
    for a in range(7):
        for b in range(7):
            v = k_ref[a, b]
            r_ref[0, a, b, 0:7] = v[:, :LANE]
            r_ref[1, a, b, 0:7, 0:64] = v[:, LANE:]
            r_ref[1, a, b, 0:7, 64:128] = v[:, LANE:]
    for b in range(7):

        def store(u, v):
            t_ref[u, b] = v
            if u == 14:
                t_ref[15, b] = pltpu.roll(v, 64, axis=1)

        to_points(evaluation(7), lambda k: r_ref[0, k, b], lambda k: r_ref[1, k, b], store)


def reversed_unit(u):
    same_sign = 2 * PAIRS - 1 - 2 * ((u - 1) // 2) + (u - 1) % 2
    paired = 19 + PAIRS - u
    return jnp.where(
        u == 0, 9, jnp.where(u < 9, same_sign, jnp.where(u == 9, 0, jnp.where(u < 14, paired, 15)))
    )


def stencil(z_ref, t_ref, s_ref, u_ref, flip):
    def row(j, carry):
        def store(u, v):
            s_ref[3, u, j] = v

        to_points(analysis(), lambda k: z_ref[0, k, j], lambda k: z_ref[1, k, j], store)
        return carry

    lax.fori_loop(0, 8, row, 0)

    def unit(u, carry):
        taps_at = reversed_unit(u) if flip else u
        rows = [s_ref[3, u, j] for j in range(8)]
        for e in range(7):
            if e != 3:
                for j in range(8):
                    s_ref[e, u, j] = shifted(rows[j], e - 3)
        acc = [None] * 8
        for e in range(7):
            taps = []
            for b in range(7):
                fb, fe = (6 - b, 6 - e) if flip else (b, e)
                taps.append(jnp.broadcast_to(t_ref[taps_at, fb, fe : fe + 1], (8, LANE)))
            for source in range(8):
                x = rows[source] if e == 3 else s_ref[e, u, source]
                for b in range(7):
                    j = source - b + 3
                    if 0 <= j < 8:
                        term = x * taps[b]
                        acc[j] = term if acc[j] is None else acc[j] + term
        for j in range(8):
            u_ref[u, j] = acc[j]
        return carry

    lax.fori_loop(0, 3 * (PAIRS + 1), unit, 0)


def fetch(sources, targets, sem):
    copies = [pltpu.make_async_copy(x, y, sem.at[i]) for i, (x, y) in enumerate(zip(sources, targets))]
    for copy in copies:
        copy.start()
    return copies


def pack_kernel(me_ref, wi_hbm, b_hbm, wo_hbm, x_hbm, out_ref, core_ref, far_ref, wi_ref, b_ref, wo_ref, x_ref, sem):
    copies = fetch((x_hbm, wi_hbm, b_hbm, wo_hbm), (x_ref, wi_ref, b_ref, wo_ref), sem)
    units = wi_ref.shape[0]
    high = (out_ref.shape[0] - 16) // 3
    out_ref[...] = jnp.zeros(out_ref.shape, BF16)
    for copy in copies:
        copy.wait()
    w_in, w_out = wi_ref[...].astype(F32), wo_ref[...].astype(F32)
    out_ref[0:units] = w_in[:, :LANE].astype(BF16)
    out_ref[high : high + units] = jnp.concatenate([w_in[:, LANE:], w_out[:, LANE:]], axis=1).astype(BF16)
    out_ref[2 * high : 2 * high + units] = w_out[:, :LANE].astype(BF16)
    line = b_ref[...].astype(F32).reshape(1, units)
    line = jnp.concatenate([line, jnp.zeros((1, LANE - units), F32)], axis=1)
    first = lax.broadcasted_iota(jnp.int32, (16, LANE), 0) == 0
    out_ref[3 * high : 3 * high + 16] = jnp.where(first, jnp.broadcast_to(line, (16, LANE)), 0.0).astype(BF16)
    odd = lax.rem(me_ref[0], 2)

    def plane(i):
        v = x_ref[i].astype(F32)
        return v.reshape(v.shape[0] * v.shape[1], v.shape[2])

    pack_planes(1 - odd, plane, core_ref)
    pack_planes(odd, plane, far_ref)


def gather_lines(lines, high):
    count = -(-len(lines) * high // LANE)
    out = [jnp.zeros((8, LANE), F32)] * count
    lane = lax.broadcasted_iota(jnp.int32, (8, LANE), 1)
    for i, line in enumerate(lines):
        at, shift = divmod(i * high, LANE)
        moved = pltpu.roll(line, shift, axis=1) if shift else line
        out[at] = out[at] + jnp.where(lane >= shift, moved, 0.0)
        if shift + high > LANE:
            out[at + 1] = out[at + 1] + jnp.where(lane < shift, moved, 0.0)
    return out


def scatter_lines(full, count, high):
    lane = lax.broadcasted_iota(jnp.int32, (8, LANE), 1)
    lines = []
    for i in range(count):
        at, shift = divmod(i * high, LANE)
        v = pltpu.roll(full[at], LANE - shift, axis=1) if shift else full[at]
        if shift + high > LANE:
            v = jnp.where(lane < LANE - shift, v, pltpu.roll(full[at + 1], LANE - shift, axis=1))
        lines.append(jnp.where(lane < high, v, 0.0))
    return lines


def prepare_kernel(*refs):
    sources, refs = refs[:9], refs[9:]
    (w_ref, z_ref, t_ref, vec_ref, xf_ref, cf_ref, db_ref), refs = refs[:7], refs[7:]
    r_ref, x_ref, c_ref, k_ref, *vec_refs, sem = refs
    copies = fetch(sources, (x_ref, c_ref, k_ref, *vec_refs, w_ref), sem)
    copies[2].wait()
    fill_taps(k_ref, r_ref, t_ref)
    for copy in copies[:2] + copies[3:]:
        copy.wait()
    rows, chans = xf_ref.shape
    for i, ref in enumerate(vec_refs):
        vec_ref[i : i + 1] = ref[...].reshape(1, chans)
    for i in range(4):
        split(x_ref[i].astype(F32), z_ref, i)
    xf_ref[...] = x_ref[...].astype(F32).reshape(rows, chans)
    cot = c_ref[...].astype(F32).reshape(rows, chans)
    cf_ref[...] = cot
    d_branch = cot * vec_ref[4:5]
    vec_ref[5:6] = jnp.sum(d_branch, axis=0, keepdims=True)
    vec_ref[6:8] = jnp.zeros((2, chans), F32)
    db_ref[...] = jnp.concatenate([d_branch, jnp.zeros((rows, 256 - chans), F32)], axis=1).astype(BF16)


def forward_kernel(last, me_ref, own_ref, p_ref, q_ref, t_ref, vec_ref, na_ref, unit_ref, s_ref, z_ref, u_ref, m_ref):
    fill_rim(last, me_ref, p_ref, q_ref, z_ref)
    z_ref[:, 3:7] = own_ref[...]
    stencil(z_ref, t_ref, s_ref, u_ref, False)

    def row(j, carry):
        main, rest = from_points(4, lambda u: u_ref[u, j])
        for i in range(4):
            at = pl.ds(pl.multiple_of(64 * i + 8 * j, 8), 8)
            m_ref[at, 0:LANE] = main[i]
            m_ref[at, LANE : LANE + 64] = rest[i][:, 0:64]
        return carry

    lax.fori_loop(0, 8, row, 0)
    chans = m_ref.shape[1]
    mixed = m_ref[...] + vec_ref[0:1]
    centred = mixed - jnp.mean(mixed, axis=-1, keepdims=True)
    inverse = lax.rsqrt(jnp.mean(centred * centred, axis=-1, keepdims=True) + 1e-06)
    unit = centred * inverse
    normed = unit * vec_ref[1:2] + vec_ref[2:3]
    rows = unit.shape[0]
    na_ref[:, 0:chans] = normed.astype(BF16)
    na_ref[:, chans:256] = jnp.zeros((rows, 256 - chans), BF16)
    unit_ref[:, 0:chans] = unit
    unit_ref[:, chans:256] = jnp.broadcast_to(inverse, (rows, 256 - chans))


def pointwise_kernel(me_ref, g0_ref, g1_ref, na_ref, unit_ref, xf_ref, cf_ref, db_ref, vec_ref, out_ref, dm_ref, core_ref, far_ref, w0_ref, w1_ref, small_ref, wi_ref, wo_ref, di_ref, do_ref, m_ref):
    rows, chans = xf_ref.shape
    normed = na_ref[...]
    d_b = db_ref[...]
    gamma = vec_ref[4:5]
    branch = jnp.zeros((rows, 256), F32)
    d_normed = jnp.zeros((rows, 256), F32)
    over_c = (((1,), (1,)), ((), ()))
    over_rows = (((0,), (0,)), ((), ()))
    pieces, high = g0_ref.shape[0], (g0_ref.shape[1] - 16) // 3
    low = low_lanes((high, LANE))
    first_row = lax.broadcasted_iota(jnp.int32, (16, LANE), 0) == 0
    for g_ref, w_ref in ((g0_ref, w0_ref), (g1_ref, w1_ref)):
        lines = []
        for i in range(pieces):
            here = slice(i * high, i * high + high)
            rest = g_ref[i, high : 2 * high].astype(F32)
            wi_ref[here, 0:LANE] = g_ref[i, 0:high]
            wi_ref[here, LANE:256] = jnp.where(low, rest, 0.0).astype(BF16)
            wo_ref[here, 0:LANE] = g_ref[i, 2 * high : 3 * high]
            wo_ref[here, LANE:256] = jnp.where(low, pltpu.roll(rest, 64, axis=1), 0.0).astype(BF16)
            line = g_ref[i, 3 * high : 3 * high + 16].astype(F32)[0:1]
            lines.append(jnp.broadcast_to(line, (8, LANE)))
        bias = gather_lines(lines, high)
        d_bias = []
        for c in range(pieces * high // LANE):
            here = slice(c * LANE, c * LANE + LANE)
            w_in, w_out = wi_ref[here], wo_ref[here]
            pre = lax.dot_general(normed, w_in, over_c, preferred_element_type=F32) + bias[c][0:1]
            d_hidden = lax.dot_general(d_b, w_out, over_c, preferred_element_type=F32)
            cdf = 0.5 * (1.0 + lax.erf(pre * root_half))
            hidden = (pre * cdf).astype(BF16)
            slope = cdf + pre * jnp.exp(-0.5 * pre * pre) * inv_root_tau
            d_pre = d_hidden * slope
            d_bias.append(jnp.broadcast_to(jnp.sum(d_pre, axis=0, keepdims=True), (8, LANE)))
            d_pre = d_pre.astype(BF16)
            branch = branch + jnp.dot(hidden, w_out, preferred_element_type=F32)
            d_normed = d_normed + jnp.dot(d_pre, w_in, preferred_element_type=F32)
            di_ref[here] = lax.dot_general(d_pre, normed, over_rows, preferred_element_type=F32)
            do_ref[here] = lax.dot_general(hidden, d_b, over_rows, preferred_element_type=F32)
        for i, line in enumerate(scatter_lines(d_bias, pieces, high)):
            here = slice(i * high, i * high + high)
            rest = jnp.where(low, di_ref[here, LANE:256], pltpu.roll(do_ref[here, LANE:256], 64, axis=1))
            w_ref[i, 0:high] = di_ref[here, 0:LANE].astype(w_ref.dtype)
            w_ref[i, high : 2 * high] = rest.astype(w_ref.dtype)
            w_ref[i, 2 * high : 3 * high] = do_ref[here, 0:LANE].astype(w_ref.dtype)
            line = jnp.where(first_row, jnp.broadcast_to(line[0:1], (16, LANE)), 0.0)
            w_ref[i, 3 * high : 3 * high + 16] = line.astype(w_ref.dtype)
    branch = branch[:, 0:chans] + vec_ref[3:4]
    out_ref[...] = (xf_ref[...] + gamma * branch).reshape(out_ref.shape).astype(BF16)
    d_normed = d_normed[:, 0:chans]
    unit = unit_ref[:, 0:chans]
    inverse = unit_ref[:, chans : chans + 1]
    scaled = d_normed * vec_ref[1:2]
    d_mixed = inverse * (
        scaled
        - jnp.mean(scaled, axis=-1, keepdims=True)
        - unit * jnp.mean(scaled * unit, axis=-1, keepdims=True)
    )
    dm_ref[...] = d_mixed.reshape(dm_ref.shape).astype(BF16)
    m_ref[...] = d_mixed.reshape(m_ref.shape)
    odd = lax.rem(me_ref[0], 2)
    pack_planes(1 - odd, lambda i: m_ref[i], core_ref)
    pack_planes(odd, lambda i: m_ref[i], far_ref)
    small_ref[...] = jnp.zeros(small_ref.shape, F32)
    sums = (d_mixed, d_normed * unit, d_normed, None, cf_ref[...] * branch)
    for i, term in enumerate(sums):
        total = vec_ref[5:6] if term is None else jnp.sum(term, axis=0, keepdims=True)
        small_ref[i : i + 1, 0:chans] = total


def rows_to_one(v):
    row = lax.broadcasted_iota(jnp.int32, (8, LANE), 0)
    v = list(v) + [jnp.zeros((8, LANE), F32)]
    for half in (4, 2, 1):
        low = (row & half) == 0
        v = [
            jnp.where(low, v[i], v[i + half])
            + jnp.where(
                low,
                pltpu.roll(v[i], 8 - half, axis=0),
                pltpu.roll(v[i + half], half, axis=0),
            )
            for i in range(half)
        ]
    return v[0]


HALF = 320


def grad_kernel(me_ref, s_ref, g_ref, small_ref, keep_ref, send_ref, z_ref, t_ref, o_ref, wa_ref, wb_ref, w_ref):
    odd = lax.rem(me_ref[0], 2)
    for i in range(4):
        split(g_ref[i].astype(F32), z_ref, i)

    def row(j, carry):
        def store(u, v):
            t_ref[u, j] = v

        to_points(evaluation(4), lambda k: z_ref[0, k, j], lambda k: z_ref[1, k, j], store)
        return carry

    lax.fori_loop(0, 8, row, 0)

    def unit(u, carry):
        grads = [t_ref[u, j] for j in range(8)]
        for e in range(7):
            acc = [None] * 7
            for source in range(8):
                x = s_ref[e, u, source]
                for b in range(7):
                    j = source - b + 3
                    if 0 <= j < 8:
                        term = x * grads[j]
                        acc[b] = term if acc[b] is None else acc[b] + term
            o_ref[u, e] = rows_to_one(acc)
        return carry

    lax.fori_loop(0, 3 * (PAIRS + 1), unit, 0)

    for b in range(49):
        at = 64 * (b // 7) + 8 * (b % 7)
        wa_ref[at : at + 8] = jnp.zeros((8, LANE), F32)
        wb_ref[at : at + 8] = jnp.zeros((8, LANE), F32)
    for e in range(7):
        main, rest = from_points(7, lambda u: o_ref[u, e])
        for a in range(7):
            wa_ref[pl.ds(a * 64 + e, 8, stride=8), :] = main[a]
            one = jnp.where(low_lanes((8, LANE)), rest[a], pltpu.roll(rest[a], 64, axis=1))
            wb_ref[pl.ds(a * 64 + e, 8, stride=8), :] = one

    low = lax.broadcasted_iota(jnp.int32, (56, LANE), 1) < 64
    for a in range(5):
        w_ref[0, 56 * a : 56 * a + 56] = wa_ref[64 * a : 64 * a + 56]
    w_ref[0, 280:288] = small_ref[:, 0:LANE]
    w_ref[0, 288:HALF] = jnp.zeros((HALF - 288, LANE), F32)
    for a in range(5, 7):
        w_ref[1, 56 * (a - 5) : 56 * (a - 5) + 56] = wa_ref[64 * a : 64 * a + 56]
    for a in range(3):
        w_ref[1, 112 + 56 * a : 168 + 56 * a] = jnp.where(
            low, wb_ref[64 * a : 64 * a + 56], wb_ref[64 * (a + 4) : 64 * (a + 4) + 56]
        )
    w_ref[1, 280:312] = jnp.where(low[0:32], wb_ref[192:224], wb_ref[224:256])
    w_ref[1, 312:320] = small_ref[:, LANE:256]
    keep_ref[...] = w_ref[odd]
    send_ref[...] = w_ref[1 - odd].astype(BF16)


def unpack_kernel(scale, me_ref, mine_ref, other_ref, dk_ref, *refs):
    odd, small_refs, w_ref = lax.rem(me_ref[0], 2), refs[:5], refs[5]
    w_ref[odd] = mine_ref[...].astype(F32) * scale
    w_ref[1 - odd] = other_ref[...].astype(F32) * scale
    for a in range(7):
        for b in range(7):
            row = 56 * a + 8 * b if a < 5 else 56 * (a - 5) + 8 * b
            main = w_ref[0 if a < 5 else 1, row : row + 7]
            if a == 3:
                at, lane = 280 + 8 * (b % 4), 64 * (b // 4)
            else:
                at, lane = 112 + 56 * (a % 4) + 8 * b, 64 * (a // 4)
            rest = w_ref[1, at : at + 7]
            dk_ref[a, b, :, 0:LANE] = main
            dk_ref[a, b, :, LANE : LANE + 64] = rest[:, lane : lane + 64]
    for i, ref in enumerate(small_refs):
        ref[:, 0:LANE] = w_ref[0, 280 + i : 281 + i]
        ref[:, LANE : LANE + 64] = w_ref[1, 312 + i : 313 + i, 0:64]


def finish_kernel(scale, a_ref, b_ref, wi_ref, bi_ref, wo_ref):
    total = (a_ref[...] + b_ref[...].astype(F32)) * scale
    units = wi_ref.shape[0]
    high = (total.shape[0] - 16) // 3
    rest = total[high : high + units]
    wi_ref[:, 0:LANE] = total[0:units]
    wi_ref[:, LANE : LANE + 64] = rest[:, 0:64]
    wo_ref[:, 0:LANE] = total[2 * high : 2 * high + units]
    wo_ref[:, LANE : LANE + 64] = rest[:, 64:LANE]
    bi_ref[...] = total[3 * high : 3 * high + 1, 0:units]


def back_kernel(last, me_ref, g_ref, p_ref, q_ref, t_ref, c_ref, dx_ref, z_ref, s_ref, u_ref):
    fill_rim(last, me_ref, p_ref, q_ref, z_ref)
    for i in range(4):
        split(g_ref[i].astype(F32), z_ref, 3 + i)
    stencil(z_ref, t_ref, s_ref, u_ref, True)
    main, rest = from_points(4, lambda u: u_ref[u], 6)
    for i in range(4):
        cot = c_ref[64 * i : 64 * i + 64].reshape(8, 8, c_ref.shape[1])
        dx_ref[i, :, :, 0:LANE] = (cot[:, :, 0:LANE] + main[i]).astype(BF16)
        dx_ref[i, :, :, LANE : LANE + 64] = (cot[:, :, LANE:] + rest[i][:, :, 0:64]).astype(BF16)


def params(mib):
    return pltpu.CompilerParams(vmem_limit_bytes=mib * 1024 * 1024)


def cost(us):
    return pl.CostEstimate(flops=int(us * 1.0e9), bytes_accessed=0, transcendentals=0)


def struct(shape, dtype):
    return jax.ShapeDtypeStruct(shape, dtype)


def on_device(
    features, cotangent, kernel, b_dw, ln_gain, ln_bias, w_in_t, b_in, w_out, b_out, gamma
):
    size_x, size_y, size_z, chans = features.shape
    devices = lax.axis_size("space")
    scale = float(size_x * devices * size_y * size_z) ** (-0.5)
    rows = size_x * size_y * size_z
    units = w_in_t.shape[0]
    bits = [1 << i for i in range(devices.bit_length() - 1)]
    order = bits
    me = lax.axis_index("space").astype(jnp.int32).reshape(1)
    def call(body, name, us, mib, out_shape, operands, scratch=(), spec=VMEM):
        specs = [SMEM if x is me else spec for x in operands]
        return pl.pallas_call(
            body,
            out_shape=out_shape,
            in_specs=specs,
            out_specs=jax.tree.map(lambda _: VMEM, out_shape),
            scratch_shapes=list(scratch),
            compiler_params=params(mib),
            name=name,
            cost_estimate=cost(us),
        )(*operands)

    z_scratch = pltpu.VMEM((2, 10, size_y, size_z, LANE), F32)
    u_scratch = pltpu.VMEM((15, size_y, size_z, LANE), F32)
    shifts = (7, 15, size_y, size_z, LANE)
    cells = struct((rows, chans), F32)

    high = -(-units // 16) * 16
    lines = 3 * high + 16
    rim = struct((3 * size_y * size_z * 3 // 2, LANE), BF16)
    raw = (w_in_t, b_in, w_out, features)
    piece, to_core, to_far = call(
        pack_kernel,
        "pack",
        1.0,
        56,
        (struct((lines, LANE), BF16), rim, rim),
        (me,) + raw,
        [pltpu.VMEM(x.shape, x.dtype) for x in raw] + [pltpu.SemaphoreType.DMA((4,))],
        HBM,
    )
    x_core, x_far = swap(to_core, 1), swap_odd(to_far)
    weights = swap(piece, order[-1])
    given = (features, cotangent, kernel, b_dw, ln_gain, ln_bias, b_out, gamma, piece)
    prepared = call(
        prepare_kernel,
        "prepare",
        1.0,
        6,
        (
            struct((lines, LANE), BF16),
            struct((2, 4, size_y, size_z, LANE), F32),
            struct((16, 7, 8, LANE), F32),
            struct((8, chans), F32),
            cells,
            cells,
            struct((rows, 256), BF16),
        ),
        given,
        [pltpu.VMEM((2, 7, 7, 8, LANE), F32)]
        + [pltpu.VMEM(x.shape, x.dtype) for x in given[:-1]]
        + [pltpu.SemaphoreType.DMA((len(given),))],
        HBM,
    )
    weights, x_core, prepared = lax.optimization_barrier((weights, x_core, prepared))
    piece, own, taps, vecs, x_f32, cot_f32, d_branch = prepared
    weights = jnp.stack([piece, weights])
    for bit in order[-2:1:-1]:
        weights = jnp.concatenate([weights, swap(weights, bit)], axis=0)
    weights, x_far = lax.optimization_barrier((weights, x_far))
    weights = jnp.concatenate([weights, swap(weights, order[1])], axis=0)
    forward = call(
        functools.partial(forward_kernel, devices - 1),
        "forward_stencil",
        2.5,
        10,
        (struct((rows, 256), BF16), struct((rows, 256), F32), struct(shifts, F32)),
        (me, own, x_core, x_far, taps, vecs),
        [z_scratch, u_scratch, pltpu.VMEM((rows, chans), F32)],
    )
    weights, forward = lax.optimization_barrier((weights, forward))
    normed, unit, shifted_x = forward
    weights_other = swap(weights, 1)

    pieces = weights.shape[0]
    output, d_mixed, to_core, to_far, grad_keep, grad_send, small = call(
        pointwise_kernel,
        "pointwise",
        2.5,
        16,
        (
            struct(features.shape, BF16),
            struct(features.shape, BF16),
            rim,
            rim,
            struct((pieces, lines, LANE), F32),
            struct((pieces, lines, LANE), BF16),
            struct((8, 256), F32),
        ),
        (me, weights, weights_other, normed, unit, x_f32, cot_f32, d_branch, vecs),
        [pltpu.VMEM((pieces * high, 256), BF16)] * 2
        + [pltpu.VMEM((pieces * high, 256), F32)] * 2
        + [pltpu.VMEM((size_x, size_y * size_z, chans), F32)],
    )
    keep, send = call(
        grad_kernel,
        "kernel_gradient",
        2.0,
        10,
        (struct((HALF, LANE), F32), struct((HALF, LANE), BF16)),
        (me, shifted_x, d_mixed, small),
        [
            pltpu.VMEM((2, 4, size_y, size_z, LANE), F32),
            u_scratch,
            pltpu.VMEM((15, 7, 8, LANE), F32),
            pltpu.VMEM((448, LANE), F32),
            pltpu.VMEM((448, LANE), F32),
            pltpu.VMEM((2, HALF, LANE), F32),
        ],
    )

    total = (grad_keep + swap(grad_send, 1).astype(F32)).reshape(pieces * lines, LANE)
    sums = keep + swap(send, 1).astype(F32)
    sums, to_core, to_far = lax.optimization_barrier((sums, to_core, to_far))
    g_core, g_far = swap(to_core, 1), swap_odd(to_far)
    for step, bit in enumerate(order[1:]):
        n = total.shape[0] // 2
        mine, kept = sums.astype(BF16), total[:n]
        got = swap(jnp.concatenate([mine, total[n:].astype(BF16)], axis=0), bit)
        if step == len(order) - 3:
            got, g_core, g_far = lax.optimization_barrier((got, g_core, g_far))
            d_x = call(
                functools.partial(back_kernel, devices - 1),
                "backward_stencil",
                2.5,
                10,
                struct(features.shape, BF16),
                (me, d_mixed, g_core, g_far, taps, cot_f32),
                [z_scratch, pltpu.VMEM(shifts, F32), u_scratch],
            )
        if step == len(order) - 2:
            got, d_x = lax.optimization_barrier((got, d_x))
        sums = mine.astype(F32) + got[:HALF].astype(F32)
        got = got[HALF:]
        total = kept + got.astype(F32)
    mine = sums.astype(BF16)
    other = swap(mine, 1)
    d_w_in, d_b_in, d_w_out = call(
        functools.partial(finish_kernel, scale),
        "finish",
        0.7,
        4,
        (struct((units, chans), F32), struct((1, units), F32), struct((units, chans), F32)),
        (kept, got),
    )
    d_kernel, *vectors = call(
        functools.partial(unpack_kernel, scale),
        "unpack",
        0.9,
        4,
        (struct(kernel.shape, F32),) + (struct((1, chans), F32),) * 5,
        (me, mine, other),
        [pltpu.VMEM((2, HALF, LANE), F32)],
    )
    d_b_dw, d_ln_gain, d_ln_bias, d_b_out, d_gamma = [v.reshape(chans) for v in vectors]
    return (
        output,
        d_x,
        d_kernel,
        d_b_dw,
        d_ln_gain,
        d_ln_bias,
        d_w_in,
        d_b_in.reshape(units),
        d_w_out,
        d_b_out,
        d_gamma,
    )


def solution(mesh):
    in_specs = (
        P(("crop", "space"), None, None, None),
        P(("crop", "space"), None, None, None),
        P(),
        P(),
        P(),
        P(),
        P("space", None),
        P("space"),
        P("space", None),
        P(),
        P(),
    )
    out_specs = (
        P(("crop", "space"), None, None, None),
        P(("crop", "space"), None, None, None),
        P("crop", None, None, None),
        P("crop"),
        P("crop"),
        P("crop"),
        P(("crop", "space"), None),
        P(("crop", "space")),
        P(("crop", "space"), None),
        P("crop"),
        P("crop"),
    )
    return jax.shard_map(
        on_device, mesh=mesh, in_specs=in_specs, out_specs=out_specs, check_vma=False
    )
```

```python
import functools

import jax
import jax.numpy as jnp
import numpy as np
from jax import lax
from jax.experimental import pallas as pl
from jax.experimental.pallas import tpu as pltpu
from jax.sharding import PartitionSpec as P

root_half = 0.7071067811865476
inv_root_tau = 0.3989422804014327
F32 = jnp.float32
BF16 = jnp.bfloat16
LANE = 128
VMEM = pl.BlockSpec(memory_space=pltpu.VMEM)
HBM = pl.BlockSpec(memory_space=pltpu.HBM)
SMEM = pl.BlockSpec(memory_space=pltpu.SMEM)

POINTS = (0.4, 0.8, 1.25, 2.5)
PAIRS = len(POINTS)


def analysis():
    finite = [0.0] + [sign * p for p in POINTS for sign in (1.0, -1.0)]
    vander = np.array([[x**k for k in range(10)] for x in finite] + [[0.0] * 9 + [1.0]])
    inverse = np.linalg.inv(vander).T
    even = [{k: float(inverse[1 + 2 * q, k]) for k in (2, 4, 6, 8)} for q in range(PAIRS)]
    odd = [{k: float(inverse[1 + 2 * q, k]) for k in (1, 3, 5, 7)} for q in range(PAIRS)]
    zero = {k: float(inverse[0, k]) for k in (0, 2, 4, 6, 8)}
    infinity = {k: float(inverse[9, k]) for k in (1, 3, 5, 7, 9)}
    return even, odd, zero, infinity


def evaluation(size):
    even = [{k: p**k for k in range(0, size, 2)} for p in POINTS]
    odd = [{k: p**k for k in range(1, size, 2)} for p in POINTS]
    return even, odd, {0: 1.0}, {size - 1: 1.0}


def weighted(load, weights):
    total = None
    for k, w in weights.items():
        term = load(k) if w == 1.0 else load(k) * w
        total = term if total is None else total + term
    return total


def low_lanes(shape):
    return lax.broadcasted_iota(jnp.int32, shape, len(shape) - 1) < 64


def to_points(tables, main, rest, store):
    even, odd, zero, infinity = tables
    for q in range(PAIRS):
        e, o = weighted(main, even[q]), weighted(main, odd[q])
        store(1 + 2 * q, e + o)
        store(2 + 2 * q, e - o)
        e, o = weighted(rest, even[q]), weighted(rest, odd[q])
        store(10 + q, jnp.where(low_lanes(e.shape), e + o, e - o))
    store(0, weighted(main, zero))
    store(9, weighted(main, infinity))
    z, i = weighted(rest, zero), weighted(rest, infinity)
    store(14, jnp.where(low_lanes(z.shape), z, i))


def from_points(size, load, power=0):
    main, rest = [None] * size, [None] * size

    def add(into, k, v, w):
        term = v if w == 1.0 else v * w
        into[k] = term if into[k] is None else into[k] + term

    for q in range(PAIRS):
        plus, minus, both = load(1 + 2 * q), load(2 + 2 * q), load(10 + q)
        swapped = pltpu.roll(both, 64, axis=both.ndim - 1)
        sums = (plus + minus, both + swapped), (plus - minus, both - swapped)
        for k in range(size):
            m, r = sums[k % 2]
            add(main, k, m, POINTS[q] ** (k + power))
            add(rest, k, r, POINTS[q] ** (k + power))
    ends = load(14)
    add(main, 0, load(0), 1.0)
    add(rest, 0, ends, 1.0)
    add(main, size - 1, load(9), 1.0)
    add(rest, size - 1, pltpu.roll(ends, 64, axis=ends.ndim - 1), 1.0)
    return main, rest


def swap(x, bit):
    size = lax.axis_size("space")
    return lax.ppermute(x, "space", [(i, i ^ bit) for i in range(size)])


def swap_odd(x):
    size = lax.axis_size("space")
    return lax.ppermute(x, "space", [(i, (i + 1 if i % 2 else i - 1) % size) for i in range(size)])


def shifted(v, by):
    if by == 0:
        return v
    row = lax.broadcasted_iota(jnp.int32, v.shape, 0)
    keep = (row < 8 - by) if by > 0 else (row >= -by)
    return jnp.where(keep, pltpu.roll(v, (-by) % 8, axis=0), 0.0)


def split(v, z_ref, plane):
    z_ref[0, plane] = v[..., :LANE]
    z_ref[1, plane, ..., 0:64] = v[..., LANE:]
    z_ref[1, plane, ..., 64:128] = v[..., LANE:]


def pack_planes(first, load, out_ref):
    for k in range(3):
        v = load(first + k)
        cells = v.shape[0]
        at = k * cells * 3 // 2
        out_ref[at : at + cells] = v[:, :LANE].astype(BF16)
        pair = jnp.concatenate([v[: cells // 2, LANE:], v[cells // 2 :, LANE:]], axis=1)
        out_ref[at + cells : at + cells * 3 // 2] = pair.astype(BF16)


def fill_rim(last, me_ref, p_ref, q_ref, z_ref):
    me = me_ref[0]
    odd = lax.rem(me, 2) == 1
    p, q = p_ref[...].astype(F32), q_ref[...].astype(F32)
    before = jnp.where(me == 0, 0.0, jnp.where(odd, p, q))
    after = jnp.where(me == last, 0.0, jnp.where(odd, q, p))
    rows, cols = z_ref.shape[2], z_ref.shape[3]
    cells = rows * cols
    for k in range(3):
        at = k * cells * 3 // 2
        for v, plane in ((before, k), (after, k + 7)):
            z_ref[0, plane] = v[at : at + cells].reshape(rows, cols, LANE)
            pair = v[at + cells : at + cells * 3 // 2]
            swapped = pltpu.roll(pair, 64, axis=1)
            low = low_lanes(pair.shape)
            z_ref[1, plane, : rows // 2] = jnp.where(low, pair, swapped).reshape(rows // 2, cols, LANE)
            z_ref[1, plane, rows // 2 :] = jnp.where(low, swapped, pair).reshape(rows // 2, cols, LANE)


def fill_taps(k_ref, r_ref, t_ref):
    for a in range(7):
        for b in range(7):
            v = k_ref[a, b]
            r_ref[0, a, b, 0:7] = v[:, :LANE]
            r_ref[1, a, b, 0:7, 0:64] = v[:, LANE:]
            r_ref[1, a, b, 0:7, 64:128] = v[:, LANE:]
    for b in range(7):

        def store(u, v):
            t_ref[u, b] = v
            if u == 14:
                t_ref[15, b] = pltpu.roll(v, 64, axis=1)

        to_points(evaluation(7), lambda k: r_ref[0, k, b], lambda k: r_ref[1, k, b], store)


def reversed_unit(u):
    same_sign = 2 * PAIRS - 1 - 2 * ((u - 1) // 2) + (u - 1) % 2
    paired = 19 + PAIRS - u
    return jnp.where(
        u == 0, 9, jnp.where(u < 9, same_sign, jnp.where(u == 9, 0, jnp.where(u < 14, paired, 15)))
    )


def stencil(z_ref, t_ref, s_ref, u_ref, flip):
    def row(j, carry):
        def store(u, v):
            s_ref[3, u, j] = v

        to_points(analysis(), lambda k: z_ref[0, k, j], lambda k: z_ref[1, k, j], store)
        return carry

    lax.fori_loop(0, 8, row, 0)

    def unit(u, carry):
        taps_at = reversed_unit(u) if flip else u
        rows = [s_ref[3, u, j] for j in range(8)]
        for e in range(7):
            if e != 3:
                for j in range(8):
                    s_ref[e, u, j] = shifted(rows[j], e - 3)
        acc = [None] * 8
        for e in range(7):
            taps = []
            for b in range(7):
                fb, fe = (6 - b, 6 - e) if flip else (b, e)
                taps.append(jnp.broadcast_to(t_ref[taps_at, fb, fe : fe + 1], (8, LANE)))
            for source in range(8):
                x = rows[source] if e == 3 else s_ref[e, u, source]
                for b in range(7):
                    j = source - b + 3
                    if 0 <= j < 8:
                        term = x * taps[b]
                        acc[j] = term if acc[j] is None else acc[j] + term
        for j in range(8):
            u_ref[u, j] = acc[j]
        return carry

    lax.fori_loop(0, 3 * (PAIRS + 1), unit, 0)


def fetch(sources, targets, sem):
    copies = [pltpu.make_async_copy(x, y, sem.at[i]) for i, (x, y) in enumerate(zip(sources, targets))]
    for copy in copies:
        copy.start()
    return copies


def pack_kernel(me_ref, wi_hbm, b_hbm, wo_hbm, x_hbm, out_ref, core_ref, far_ref, wi_ref, b_ref, wo_ref, x_ref, sem):
    copies = fetch((x_hbm, wi_hbm, b_hbm, wo_hbm), (x_ref, wi_ref, b_ref, wo_ref), sem)
    units = wi_ref.shape[0]
    high = (out_ref.shape[0] - 16) // 3
    out_ref[...] = jnp.zeros(out_ref.shape, BF16)
    for copy in copies:
        copy.wait()
    w_in, w_out = wi_ref[...].astype(F32), wo_ref[...].astype(F32)
    out_ref[0:units] = w_in[:, :LANE].astype(BF16)
    out_ref[high : high + units] = jnp.concatenate([w_in[:, LANE:], w_out[:, LANE:]], axis=1).astype(BF16)
    out_ref[2 * high : 2 * high + units] = w_out[:, :LANE].astype(BF16)
    line = b_ref[...].astype(F32).reshape(1, units)
    line = jnp.concatenate([line, jnp.zeros((1, LANE - units), F32)], axis=1)
    first = lax.broadcasted_iota(jnp.int32, (16, LANE), 0) == 0
    out_ref[3 * high : 3 * high + 16] = jnp.where(first, jnp.broadcast_to(line, (16, LANE)), 0.0).astype(BF16)
    odd = lax.rem(me_ref[0], 2)

    def plane(i):
        v = x_ref[i].astype(F32)
        return v.reshape(v.shape[0] * v.shape[1], v.shape[2])

    pack_planes(1 - odd, plane, core_ref)
    pack_planes(odd, plane, far_ref)


def gather_lines(lines, high):
    count = -(-len(lines) * high // LANE)
    out = [jnp.zeros((8, LANE), F32)] * count
    lane = lax.broadcasted_iota(jnp.int32, (8, LANE), 1)
    for i, line in enumerate(lines):
        at, shift = divmod(i * high, LANE)
        moved = pltpu.roll(line, shift, axis=1) if shift else line
        out[at] = out[at] + jnp.where(lane >= shift, moved, 0.0)
        if shift + high > LANE:
            out[at + 1] = out[at + 1] + jnp.where(lane < shift, moved, 0.0)
    return out


def scatter_lines(full, count, high):
    lane = lax.broadcasted_iota(jnp.int32, (8, LANE), 1)
    lines = []
    for i in range(count):
        at, shift = divmod(i * high, LANE)
        v = pltpu.roll(full[at], LANE - shift, axis=1) if shift else full[at]
        if shift + high > LANE:
            v = jnp.where(lane < LANE - shift, v, pltpu.roll(full[at + 1], LANE - shift, axis=1))
        lines.append(jnp.where(lane < high, v, 0.0))
    return lines


def prepare_kernel(*refs):
    sources, refs = refs[:9], refs[9:]
    (w_ref, z_ref, t_ref, vec_ref, xf_ref, cf_ref, db_ref), refs = refs[:7], refs[7:]
    r_ref, x_ref, c_ref, k_ref, *vec_refs, sem = refs
    copies = fetch(sources, (x_ref, c_ref, k_ref, *vec_refs, w_ref), sem)
    copies[2].wait()
    fill_taps(k_ref, r_ref, t_ref)
    for copy in copies[:2] + copies[3:]:
        copy.wait()
    rows, chans = xf_ref.shape
    for i, ref in enumerate(vec_refs):
        vec_ref[i : i + 1] = ref[...].reshape(1, chans)
    for i in range(4):
        split(x_ref[i].astype(F32), z_ref, i)
    xf_ref[...] = x_ref[...].astype(F32).reshape(rows, chans)
    cot = c_ref[...].astype(F32).reshape(rows, chans)
    cf_ref[...] = cot
    d_branch = cot * vec_ref[4:5]
    vec_ref[5:6] = jnp.sum(d_branch, axis=0, keepdims=True)
    vec_ref[6:8] = jnp.zeros((2, chans), F32)
    db_ref[...] = jnp.concatenate([d_branch, jnp.zeros((rows, 256 - chans), F32)], axis=1).astype(BF16)


def forward_kernel(last, me_ref, own_ref, p_ref, q_ref, t_ref, vec_ref, na_ref, unit_ref, s_ref, z_ref, u_ref, m_ref):
    fill_rim(last, me_ref, p_ref, q_ref, z_ref)
    z_ref[:, 3:7] = own_ref[...]
    stencil(z_ref, t_ref, s_ref, u_ref, False)

    def row(j, carry):
        main, rest = from_points(4, lambda u: u_ref[u, j])
        for i in range(4):
            at = pl.ds(pl.multiple_of(64 * i + 8 * j, 8), 8)
            m_ref[at, 0:LANE] = main[i]
            m_ref[at, LANE : LANE + 64] = rest[i][:, 0:64]
        return carry

    lax.fori_loop(0, 8, row, 0)
    chans = m_ref.shape[1]
    mixed = m_ref[...] + vec_ref[0:1]
    centred = mixed - jnp.mean(mixed, axis=-1, keepdims=True)
    inverse = lax.rsqrt(jnp.mean(centred * centred, axis=-1, keepdims=True) + 1e-06)
    unit = centred * inverse
    normed = unit * vec_ref[1:2] + vec_ref[2:3]
    rows = unit.shape[0]
    na_ref[:, 0:chans] = normed.astype(BF16)
    na_ref[:, chans:256] = jnp.zeros((rows, 256 - chans), BF16)
    unit_ref[:, 0:chans] = unit
    unit_ref[:, chans:256] = jnp.broadcast_to(inverse, (rows, 256 - chans))


def pointwise_kernel(me_ref, g0_ref, g1_ref, na_ref, unit_ref, xf_ref, cf_ref, db_ref, vec_ref, branch_ref, dm_ref, core_ref, far_ref, w0_ref, w1_ref, small_ref, wi_ref, wo_ref, di_ref, do_ref, m_ref):
    rows, chans = xf_ref.shape
    normed = na_ref[...]
    d_b = db_ref[...]
    gamma = vec_ref[4:5]
    branch = jnp.zeros((rows, 256), F32)
    d_normed = jnp.zeros((rows, 256), F32)
    over_c = (((1,), (1,)), ((), ()))
    over_rows = (((0,), (0,)), ((), ()))
    pieces, high = g0_ref.shape[0], (g0_ref.shape[1] - 16) // 3
    low = low_lanes((high, LANE))
    first_row = lax.broadcasted_iota(jnp.int32, (16, LANE), 0) == 0
    for g_ref, w_ref in ((g0_ref, w0_ref), (g1_ref, w1_ref)):
        lines = []
        for i in range(pieces):
            here = slice(i * high, i * high + high)
            rest = g_ref[i, high : 2 * high].astype(F32)
            wi_ref[here, 0:LANE] = g_ref[i, 0:high]
            wi_ref[here, LANE:256] = jnp.where(low, rest, 0.0).astype(BF16)
            wo_ref[here, 0:LANE] = g_ref[i, 2 * high : 3 * high]
            wo_ref[here, LANE:256] = jnp.where(low, pltpu.roll(rest, 64, axis=1), 0.0).astype(BF16)
            line = g_ref[i, 3 * high : 3 * high + 16].astype(F32)[0:1]
            lines.append(jnp.broadcast_to(line, (8, LANE)))
        bias = gather_lines(lines, high)
        d_bias = []
        for c in range(pieces * high // LANE):
            here = slice(c * LANE, c * LANE + LANE)
            w_in, w_out = wi_ref[here], wo_ref[here]
            pre = lax.dot_general(normed, w_in, over_c, preferred_element_type=F32) + bias[c][0:1]
            d_hidden = lax.dot_general(d_b, w_out, over_c, preferred_element_type=F32)
            cdf = 0.5 * (1.0 + lax.erf(pre * root_half))
            hidden = (pre * cdf).astype(BF16)
            slope = cdf + pre * jnp.exp(-0.5 * pre * pre) * inv_root_tau
            d_pre = d_hidden * slope
            d_bias.append(jnp.broadcast_to(jnp.sum(d_pre, axis=0, keepdims=True), (8, LANE)))
            d_pre = d_pre.astype(BF16)
            branch = branch + jnp.dot(hidden, w_out, preferred_element_type=F32)
            d_normed = d_normed + jnp.dot(d_pre, w_in, preferred_element_type=F32)
            di_ref[here] = lax.dot_general(d_pre, normed, over_rows, preferred_element_type=F32)
            do_ref[here] = lax.dot_general(hidden, d_b, over_rows, preferred_element_type=F32)
        for i, line in enumerate(scatter_lines(d_bias, pieces, high)):
            here = slice(i * high, i * high + high)
            rest = jnp.where(low, di_ref[here, LANE:256], pltpu.roll(do_ref[here, LANE:256], 64, axis=1))
            w_ref[i, 0:high] = di_ref[here, 0:LANE].astype(w_ref.dtype)
            w_ref[i, high : 2 * high] = rest.astype(w_ref.dtype)
            w_ref[i, 2 * high : 3 * high] = do_ref[here, 0:LANE].astype(w_ref.dtype)
            line = jnp.where(first_row, jnp.broadcast_to(line[0:1], (16, LANE)), 0.0)
            w_ref[i, 3 * high : 3 * high + 16] = line.astype(w_ref.dtype)
    branch = branch[:, 0:chans] + vec_ref[3:4]
    branch_ref[...] = gamma * branch
    d_normed = d_normed[:, 0:chans]
    unit = unit_ref[:, 0:chans]
    inverse = unit_ref[:, chans : chans + 1]
    scaled = d_normed * vec_ref[1:2]
    d_mixed = inverse * (
        scaled
        - jnp.mean(scaled, axis=-1, keepdims=True)
        - unit * jnp.mean(scaled * unit, axis=-1, keepdims=True)
    )
    dm_ref[...] = d_mixed.reshape(dm_ref.shape).astype(BF16)
    m_ref[...] = d_mixed.reshape(m_ref.shape)
    odd = lax.rem(me_ref[0], 2)
    pack_planes(1 - odd, lambda i: m_ref[i], core_ref)
    pack_planes(odd, lambda i: m_ref[i], far_ref)
    small_ref[...] = jnp.zeros(small_ref.shape, F32)
    sums = (d_mixed, d_normed * unit, d_normed, None, cf_ref[...] * branch)
    for i, term in enumerate(sums):
        total = vec_ref[5:6] if term is None else jnp.sum(term, axis=0, keepdims=True)
        small_ref[i : i + 1, 0:chans] = total


def rows_to_one(v):
    row = lax.broadcasted_iota(jnp.int32, (8, LANE), 0)
    v = list(v) + [jnp.zeros((8, LANE), F32)]
    for half in (4, 2, 1):
        low = (row & half) == 0
        v = [
            jnp.where(low, v[i], v[i + half])
            + jnp.where(
                low,
                pltpu.roll(v[i], 8 - half, axis=0),
                pltpu.roll(v[i + half], half, axis=0),
            )
            for i in range(half)
        ]
    return v[0]


HALF = 272


def block(g):
    return 64 * (g // 7) + 8 * (g % 7)


def main_at(g):
    return (0, 7 * g) if g < 38 else (1, 7 * (g - 38))


def rest_at(g):
    return 77 + 7 * (g % 25), 64 * (g // 25)


def grad_kernel(me_ref, s_ref, g_ref, small_ref, keep_ref, send_ref, z_ref, t_ref, o_ref, wa_ref, wb_ref, w_ref):
    odd = lax.rem(me_ref[0], 2)
    for i in range(4):
        split(g_ref[i].astype(F32), z_ref, i)

    def row(j, carry):
        def store(u, v):
            t_ref[u, j] = v

        to_points(evaluation(4), lambda k: z_ref[0, k, j], lambda k: z_ref[1, k, j], store)
        return carry

    lax.fori_loop(0, 8, row, 0)

    def unit(u, carry):
        grads = [t_ref[u, j] for j in range(8)]
        for e in range(7):
            acc = [None] * 7
            for source in range(8):
                x = s_ref[e, u, source]
                for b in range(7):
                    j = source - b + 3
                    if 0 <= j < 8:
                        term = x * grads[j]
                        acc[b] = term if acc[b] is None else acc[b] + term
            o_ref[u, e] = rows_to_one(acc)
        return carry

    lax.fori_loop(0, 3 * (PAIRS + 1), unit, 0)

    for b in range(49):
        at = 64 * (b // 7) + 8 * (b % 7)
        wa_ref[at : at + 8] = jnp.zeros((8, LANE), F32)
        wb_ref[at : at + 8] = jnp.zeros((8, LANE), F32)
    for e in range(7):
        main, rest = from_points(7, lambda u: o_ref[u, e])
        for a in range(7):
            wa_ref[pl.ds(a * 64 + e, 8, stride=8), :] = main[a]
            one = jnp.where(low_lanes((8, LANE)), rest[a], pltpu.roll(rest[a], 64, axis=1))
            wb_ref[pl.ds(a * 64 + e, 8, stride=8), :] = one

    w_ref[0, HALF - 16 : HALF] = jnp.zeros((16, LANE), F32)
    w_ref[1, HALF - 16 : HALF] = jnp.zeros((16, LANE), F32)
    low = low_lanes((8, LANE))[0:7]
    for g in range(49):
        half, row = main_at(g)
        w_ref[half, row : row + 7] = wa_ref[block(g) : block(g) + 7]
        row, lane = rest_at(g)
        if lane == 0:
            pair = min(g + 25, 48)
            w_ref[1, row : row + 7] = jnp.where(
                low, wb_ref[block(g) : block(g) + 7], wb_ref[block(pair) : block(pair) + 7]
            )
    w_ref[0, 266:271] = small_ref[0:5, 0:LANE]
    w_ref[1, 252:257] = small_ref[0:5, LANE:256]
    keep_ref[...] = w_ref[odd]
    send_ref[...] = w_ref[1 - odd].astype(BF16)


def unpack_kernel(scale, me_ref, mine_ref, other_ref, dk_ref, *refs):
    odd, small_refs, w_ref = lax.rem(me_ref[0], 2), refs[:5], refs[5]
    w_ref[odd] = mine_ref[...].astype(F32) * scale
    w_ref[1 - odd] = other_ref[...].astype(F32) * scale
    for g in range(49):
        half, row = main_at(g)
        dk_ref[g // 7, g % 7, :, 0:LANE] = w_ref[half, row : row + 7]
        row, lane = rest_at(g)
        dk_ref[g // 7, g % 7, :, LANE : LANE + 64] = w_ref[1, row : row + 7][:, lane : lane + 64]
    for i, ref in enumerate(small_refs):
        ref[:, 0:LANE] = w_ref[0, 266 + i : 267 + i]
        ref[:, LANE : LANE + 64] = w_ref[1, 252 + i : 253 + i, 0:64]


def finish_kernel(scale, a_ref, b_ref, wi_ref, bi_ref, wo_ref):
    total = (a_ref[...] + b_ref[...].astype(F32)) * scale
    units = wi_ref.shape[0]
    high = (total.shape[0] - 16) // 3
    rest = total[high : high + units]
    wi_ref[:, 0:LANE] = total[0:units]
    wi_ref[:, LANE : LANE + 64] = rest[:, 0:64]
    wo_ref[:, 0:LANE] = total[2 * high : 2 * high + units]
    wo_ref[:, LANE : LANE + 64] = rest[:, 64:LANE]
    bi_ref[...] = total[3 * high : 3 * high + 1, 0:units]


def back_kernel(last, me_ref, g_ref, p_ref, q_ref, t_ref, c_ref, xf_ref, branch_ref, dx_ref, out_ref, z_ref, s_ref, u_ref):
    fill_rim(last, me_ref, p_ref, q_ref, z_ref)
    for i in range(4):
        split(g_ref[i].astype(F32), z_ref, 3 + i)
    out_ref[...] = (xf_ref[...] + branch_ref[...]).reshape(out_ref.shape).astype(BF16)
    stencil(z_ref, t_ref, s_ref, u_ref, True)
    main, rest = from_points(4, lambda u: u_ref[u], 6)
    for i in range(4):
        cot = c_ref[64 * i : 64 * i + 64].reshape(8, 8, c_ref.shape[1])
        dx_ref[i, :, :, 0:LANE] = (cot[:, :, 0:LANE] + main[i]).astype(BF16)
        dx_ref[i, :, :, LANE : LANE + 64] = (cot[:, :, LANE:] + rest[i][:, :, 0:64]).astype(BF16)


def params(mib):
    return pltpu.CompilerParams(vmem_limit_bytes=mib * 1024 * 1024)


def cost(us):
    return pl.CostEstimate(flops=int(us * 1.0e9), bytes_accessed=0, transcendentals=0)


def struct(shape, dtype):
    return jax.ShapeDtypeStruct(shape, dtype)


def on_device(
    features, cotangent, kernel, b_dw, ln_gain, ln_bias, w_in_t, b_in, w_out, b_out, gamma
):
    size_x, size_y, size_z, chans = features.shape
    devices = lax.axis_size("space")
    scale = float(size_x * devices * size_y * size_z) ** (-0.5)
    rows = size_x * size_y * size_z
    units = w_in_t.shape[0]
    bits = [1 << i for i in range(devices.bit_length() - 1)]
    order, sums_order = bits, [bits[0], bits[-1], bits[1]] + bits[2:-1]
    me = lax.axis_index("space").astype(jnp.int32).reshape(1)
    def call(body, name, us, mib, out_shape, operands, scratch=(), spec=VMEM):
        specs = [SMEM if x is me else spec for x in operands]
        return pl.pallas_call(
            body,
            out_shape=out_shape,
            in_specs=specs,
            out_specs=jax.tree.map(lambda _: VMEM, out_shape),
            scratch_shapes=list(scratch),
            compiler_params=params(mib),
            name=name,
            cost_estimate=cost(us),
        )(*operands)

    z_scratch = pltpu.VMEM((2, 10, size_y, size_z, LANE), F32)
    u_scratch = pltpu.VMEM((15, size_y, size_z, LANE), F32)
    shifts = (7, 15, size_y, size_z, LANE)
    cells = struct((rows, chans), F32)

    high = -(-units // 16) * 16
    lines = 3 * high + 16
    rim = struct((3 * size_y * size_z * 3 // 2, LANE), BF16)
    raw = (w_in_t, b_in, w_out, features)
    piece, to_core, to_far = call(
        pack_kernel,
        "pack",
        1.0,
        56,
        (struct((lines, LANE), BF16), rim, rim),
        (me,) + raw,
        [pltpu.VMEM(x.shape, x.dtype) for x in raw] + [pltpu.SemaphoreType.DMA((4,))],
        HBM,
    )
    x_core, x_far = swap(to_core, 1), swap_odd(to_far)
    weights = swap(piece, order[-1])
    given = (features, cotangent, kernel, b_dw, ln_gain, ln_bias, b_out, gamma, piece)
    prepared = call(
        prepare_kernel,
        "prepare",
        1.0,
        6,
        (
            struct((lines, LANE), BF16),
            struct((2, 4, size_y, size_z, LANE), F32),
            struct((16, 7, 8, LANE), F32),
            struct((8, chans), F32),
            cells,
            cells,
            struct((rows, 256), BF16),
        ),
        given,
        [pltpu.VMEM((2, 7, 7, 8, LANE), F32)]
        + [pltpu.VMEM(x.shape, x.dtype) for x in given[:-1]]
        + [pltpu.SemaphoreType.DMA((len(given),))],
        HBM,
    )
    weights, x_core, prepared = lax.optimization_barrier((weights, x_core, prepared))
    piece, own, taps, vecs, x_f32, cot_f32, d_branch = prepared
    weights = jnp.stack([piece, weights])
    for bit in order[-2:2:-1]:
        weights = jnp.concatenate([weights, swap(weights, bit)], axis=0)
    over_z, over_x = swap(weights, order[2]), swap(weights, order[1])
    over_z, over_x, x_far = lax.optimization_barrier((over_z, over_x, x_far))
    n = over_z.shape[0] // 2
    corner = swap(over_z[:n], order[1]), swap(over_x[n:], order[2])
    weights = jnp.concatenate([weights, over_z, over_x, *corner], axis=0)
    forward = call(
        functools.partial(forward_kernel, devices - 1),
        "forward_stencil",
        2.5,
        10,
        (struct((rows, 256), BF16), struct((rows, 256), F32), struct(shifts, F32)),
        (me, own, x_core, x_far, taps, vecs),
        [z_scratch, u_scratch, pltpu.VMEM((rows, chans), F32)],
    )
    weights, forward = lax.optimization_barrier((weights, forward))
    normed, unit, shifted_x = forward
    weights_other = swap(weights, 1)

    pieces = weights.shape[0]
    branch, d_mixed, to_core, to_far, grad_keep, grad_send, small = call(
        pointwise_kernel,
        "pointwise",
        2.5,
        16,
        (
            cells,
            struct(features.shape, BF16),
            rim,
            rim,
            struct((pieces, lines, LANE), F32),
            struct((pieces, lines, LANE), BF16),
            struct((8, 256), F32),
        ),
        (me, weights, weights_other, normed, unit, x_f32, cot_f32, d_branch, vecs),
        [pltpu.VMEM((pieces * high, 256), BF16)] * 2
        + [pltpu.VMEM((pieces * high, 256), F32)] * 2
        + [pltpu.VMEM((size_x, size_y * size_z, chans), F32)],
    )
    keep, send = call(
        grad_kernel,
        "kernel_gradient",
        2.0,
        10,
        (struct((HALF, LANE), F32), struct((HALF, LANE), BF16)),
        (me, shifted_x, d_mixed, small),
        [
            pltpu.VMEM((2, 4, size_y, size_z, LANE), F32),
            u_scratch,
            pltpu.VMEM((15, 7, 8, LANE), F32),
            pltpu.VMEM((448, LANE), F32),
            pltpu.VMEM((448, LANE), F32),
            pltpu.VMEM((2, HALF, LANE), F32),
        ],
    )

    total = (grad_keep + swap(grad_send, 1).astype(F32)).reshape(pieces * lines, LANE)
    send, to_core, to_far = lax.optimization_barrier((send, to_core, to_far))
    sums = keep + swap(send, 1).astype(F32)
    g_core, g_far = swap(to_core, 1), swap_odd(to_far)
    for step, (bit, sums_bit) in enumerate(zip(order[1:], sums_order[1:])):
        n = total.shape[0] // 2
        mine, kept = sums.astype(BF16), total[:n]
        theirs = swap(mine, sums_bit)
        got = swap(total[n:].astype(BF16), bit)
        if step == 0:
            theirs, g_core, g_far = lax.optimization_barrier((theirs, g_core, g_far))
        if step == len(order) - 3:
            d_x, output = call(
                functools.partial(back_kernel, devices - 1),
                "backward_stencil",
                2.5,
                10,
                (struct(features.shape, BF16),) * 2,
                (me, d_mixed, g_core, g_far, taps, cot_f32, x_f32, branch),
                [z_scratch, pltpu.VMEM(shifts, F32), u_scratch],
            )
            theirs, d_x, output = lax.optimization_barrier((theirs, d_x, output))
        if step < len(order) - 2:
            theirs, got = lax.optimization_barrier((theirs, got))
        sums = mine.astype(F32) + theirs.astype(F32)
        total = kept + got.astype(F32)
    mine = sums.astype(BF16)
    other = swap(mine, 1)
    d_w_in, d_b_in, d_w_out = call(
        functools.partial(finish_kernel, scale),
        "finish",
        0.7,
        4,
        (struct((units, chans), F32), struct((1, units), F32), struct((units, chans), F32)),
        (kept, got),
    )
    d_kernel, *vectors = call(
        functools.partial(unpack_kernel, scale),
        "unpack",
        0.9,
        4,
        (struct(kernel.shape, F32),) + (struct((1, chans), F32),) * 5,
        (me, mine, other),
        [pltpu.VMEM((2, HALF, LANE), F32)],
    )
    d_b_dw, d_ln_gain, d_ln_bias, d_b_out, d_gamma = [v.reshape(chans) for v in vectors]
    return (
        output,
        d_x,
        d_kernel,
        d_b_dw,
        d_ln_gain,
        d_ln_bias,
        d_w_in,
        d_b_in.reshape(units),
        d_w_out,
        d_b_out,
        d_gamma,
    )


def solution(mesh):
    in_specs = (
        P(("crop", "space"), None, None, None),
        P(("crop", "space"), None, None, None),
        P(),
        P(),
        P(),
        P(),
        P("space", None),
        P("space"),
        P("space", None),
        P(),
        P(),
    )
    out_specs = (
        P(("crop", "space"), None, None, None),
        P(("crop", "space"), None, None, None),
        P("crop", None, None, None),
        P("crop"),
        P("crop"),
        P("crop"),
        P(("crop", "space"), None),
        P(("crop", "space")),
        P(("crop", "space"), None),
        P("crop"),
        P("crop"),
    )
    return jax.shard_map(
        on_device, mesh=mesh, in_specs=in_specs, out_specs=out_specs, check_vma=False
    )
```

```python
import functools

import jax
import jax.numpy as jnp
import numpy as np
from jax import lax
from jax.experimental import pallas as pl
from jax.experimental.pallas import tpu as pltpu
from jax.sharding import PartitionSpec as P

root_half = 0.7071067811865476
inv_root_tau = 0.3989422804014327
F32 = jnp.float32
BF16 = jnp.bfloat16
LANE = 128
VMEM = pl.BlockSpec(memory_space=pltpu.VMEM)
HBM = pl.BlockSpec(memory_space=pltpu.HBM)
SMEM = pl.BlockSpec(memory_space=pltpu.SMEM)

POINTS = (0.4, 0.8, 1.25, 2.5)
PAIRS = len(POINTS)


def analysis():
    finite = [0.0] + [sign * p for p in POINTS for sign in (1.0, -1.0)]
    vander = np.array([[x**k for k in range(10)] for x in finite] + [[0.0] * 9 + [1.0]])
    inverse = np.linalg.inv(vander).T
    even = [{k: float(inverse[1 + 2 * q, k]) for k in (2, 4, 6, 8)} for q in range(PAIRS)]
    odd = [{k: float(inverse[1 + 2 * q, k]) for k in (1, 3, 5, 7)} for q in range(PAIRS)]
    zero = {k: float(inverse[0, k]) for k in (0, 2, 4, 6, 8)}
    infinity = {k: float(inverse[9, k]) for k in (1, 3, 5, 7, 9)}
    return even, odd, zero, infinity


def evaluation(size):
    even = [{k: p**k for k in range(0, size, 2)} for p in POINTS]
    odd = [{k: p**k for k in range(1, size, 2)} for p in POINTS]
    return even, odd, {0: 1.0}, {size - 1: 1.0}


def weighted(load, weights):
    total = None
    for k, w in weights.items():
        term = load(k) if w == 1.0 else load(k) * w
        total = term if total is None else total + term
    return total


def low_lanes(shape):
    return lax.broadcasted_iota(jnp.int32, shape, len(shape) - 1) < 64


def to_points(tables, main, rest, store):
    even, odd, zero, infinity = tables
    for q in range(PAIRS):
        e, o = weighted(main, even[q]), weighted(main, odd[q])
        store(1 + 2 * q, e + o)
        store(2 + 2 * q, e - o)
        e, o = weighted(rest, even[q]), weighted(rest, odd[q])
        store(10 + q, jnp.where(low_lanes(e.shape), e + o, e - o))
    store(0, weighted(main, zero))
    store(9, weighted(main, infinity))
    z, i = weighted(rest, zero), weighted(rest, infinity)
    store(14, jnp.where(low_lanes(z.shape), z, i))


def from_points(size, load, power=0):
    main, rest = [None] * size, [None] * size

    def add(into, k, v, w):
        term = v if w == 1.0 else v * w
        into[k] = term if into[k] is None else into[k] + term

    for q in range(PAIRS):
        plus, minus, both = load(1 + 2 * q), load(2 + 2 * q), load(10 + q)
        swapped = pltpu.roll(both, 64, axis=both.ndim - 1)
        sums = (plus + minus, both + swapped), (plus - minus, both - swapped)
        for k in range(size):
            m, r = sums[k % 2]
            add(main, k, m, POINTS[q] ** (k + power))
            add(rest, k, r, POINTS[q] ** (k + power))
    ends = load(14)
    add(main, 0, load(0), 1.0)
    add(rest, 0, ends, 1.0)
    add(main, size - 1, load(9), 1.0)
    add(rest, size - 1, pltpu.roll(ends, 64, axis=ends.ndim - 1), 1.0)
    return main, rest


def swap(x, bit):
    size = lax.axis_size("space")
    return lax.ppermute(x, "space", [(i, i ^ bit) for i in range(size)])


def swap_odd(x):
    size = lax.axis_size("space")
    return lax.ppermute(x, "space", [(i, (i + 1 if i % 2 else i - 1) % size) for i in range(size)])


def shifted(v, by):
    if by == 0:
        return v
    row = lax.broadcasted_iota(jnp.int32, v.shape, 0)
    keep = (row < 8 - by) if by > 0 else (row >= -by)
    return jnp.where(keep, pltpu.roll(v, (-by) % 8, axis=0), 0.0)


def split(v, z_ref, plane):
    z_ref[0, plane] = v[..., :LANE]
    z_ref[1, plane, ..., 0:64] = v[..., LANE:]
    z_ref[1, plane, ..., 64:128] = v[..., LANE:]


def pack_planes(first, load, out_ref, base=0):
    for k in range(3):
        v = load(first + k)
        cells = v.shape[0]
        at = base + k * cells * 3 // 2
        out_ref[at : at + cells] = v[:, :LANE].astype(BF16)
        pair = jnp.concatenate([v[: cells // 2, LANE:], v[cells // 2 :, LANE:]], axis=1)
        out_ref[at + cells : at + cells * 3 // 2] = pair.astype(BF16)


def fill_rim(last, me_ref, p_ref, q_ref, z_ref):
    me = me_ref[0]
    odd = lax.rem(me, 2) == 1
    p, q = p_ref[...].astype(F32), q_ref[...].astype(F32)
    before = jnp.where(me == 0, 0.0, jnp.where(odd, p, q))
    after = jnp.where(me == last, 0.0, jnp.where(odd, q, p))
    rows, cols = z_ref.shape[2], z_ref.shape[3]
    cells = rows * cols
    for k in range(3):
        at = k * cells * 3 // 2
        for v, plane in ((before, k), (after, k + 7)):
            z_ref[0, plane] = v[at : at + cells].reshape(rows, cols, LANE)
            pair = v[at + cells : at + cells * 3 // 2]
            swapped = pltpu.roll(pair, 64, axis=1)
            low = low_lanes(pair.shape)
            z_ref[1, plane, : rows // 2] = jnp.where(low, pair, swapped).reshape(rows // 2, cols, LANE)
            z_ref[1, plane, rows // 2 :] = jnp.where(low, swapped, pair).reshape(rows // 2, cols, LANE)


def fill_taps(k_ref, r_ref, t_ref):
    for a in range(7):
        for b in range(7):
            v = k_ref[a, b]
            r_ref[0, a, b, 0:7] = v[:, :LANE]
            r_ref[1, a, b, 0:7, 0:64] = v[:, LANE:]
            r_ref[1, a, b, 0:7, 64:128] = v[:, LANE:]
    for b in range(7):

        def store(u, v):
            t_ref[u, b] = v
            if u == 14:
                t_ref[15, b] = pltpu.roll(v, 64, axis=1)

        to_points(evaluation(7), lambda k: r_ref[0, k, b], lambda k: r_ref[1, k, b], store)


def reversed_unit(u):
    same_sign = 2 * PAIRS - 1 - 2 * ((u - 1) // 2) + (u - 1) % 2
    paired = 19 + PAIRS - u
    return jnp.where(
        u == 0, 9, jnp.where(u < 9, same_sign, jnp.where(u == 9, 0, jnp.where(u < 14, paired, 15)))
    )


def stencil(z_ref, t_ref, s_ref, u_ref, flip):
    def row(j, carry):
        def store(u, v):
            s_ref[3, u, j] = v

        to_points(analysis(), lambda k: z_ref[0, k, j], lambda k: z_ref[1, k, j], store)
        return carry

    lax.fori_loop(0, 8, row, 0, unroll=8)

    def unit(u, carry):
        taps_at = reversed_unit(u) if flip else u
        rows = [s_ref[3, u, j] for j in range(8)]
        for e in range(7):
            if e != 3:
                for j in range(8):
                    s_ref[e, u, j] = shifted(rows[j], e - 3)
        acc = [None] * 8
        for e in range(7):
            taps = []
            for b in range(7):
                fb, fe = (6 - b, 6 - e) if flip else (b, e)
                taps.append(jnp.broadcast_to(t_ref[taps_at, fb, fe : fe + 1], (8, LANE)))
            for source in range(8):
                x = rows[source] if e == 3 else s_ref[e, u, source]
                for b in range(7):
                    j = source - b + 3
                    if 0 <= j < 8:
                        term = x * taps[b]
                        acc[j] = term if acc[j] is None else acc[j] + term
        for j in range(8):
            u_ref[u, j] = acc[j]
        return carry

    lax.fori_loop(0, 3 * (PAIRS + 1), unit, 0, unroll=3)


def fetch(sources, targets, sem):
    copies = [pltpu.make_async_copy(x, y, sem.at[i]) for i, (x, y) in enumerate(zip(sources, targets))]
    for copy in copies:
        copy.start()
    return copies


def pack_kernel(me_ref, wi_hbm, b_hbm, wo_hbm, x_hbm, out_ref, core_ref, far_ref, wi_ref, b_ref, wo_ref, x_ref, sem):
    copies = fetch((x_hbm, wi_hbm, b_hbm, wo_hbm), (x_ref, wi_ref, b_ref, wo_ref), sem)
    units = wi_ref.shape[0]
    high = (out_ref.shape[0] - 16) // 3
    out_ref[...] = jnp.zeros(out_ref.shape, BF16)
    for copy in copies:
        copy.wait()
    w_in, w_out = wi_ref[...].astype(F32), wo_ref[...].astype(F32)
    out_ref[0:units] = w_in[:, :LANE].astype(BF16)
    out_ref[high : high + units] = jnp.concatenate([w_in[:, LANE:], w_out[:, LANE:]], axis=1).astype(BF16)
    out_ref[2 * high : 2 * high + units] = w_out[:, :LANE].astype(BF16)
    line = b_ref[...].astype(F32).reshape(1, units)
    line = jnp.concatenate([line, jnp.zeros((1, LANE - units), F32)], axis=1)
    first = lax.broadcasted_iota(jnp.int32, (16, LANE), 0) == 0
    out_ref[3 * high : 3 * high + 16] = jnp.where(first, jnp.broadcast_to(line, (16, LANE)), 0.0).astype(BF16)
    odd = lax.rem(me_ref[0], 2)

    def plane(i):
        v = x_ref[i].astype(F32)
        return v.reshape(v.shape[0] * v.shape[1], v.shape[2])

    pack_planes(1 - odd, plane, core_ref)
    pack_planes(odd, plane, far_ref)


def gather_lines(lines, high):
    count = -(-len(lines) * high // LANE)
    out = [jnp.zeros((8, LANE), F32)] * count
    lane = lax.broadcasted_iota(jnp.int32, (8, LANE), 1)
    for i, line in enumerate(lines):
        at, shift = divmod(i * high, LANE)
        moved = pltpu.roll(line, shift, axis=1) if shift else line
        out[at] = out[at] + jnp.where(lane >= shift, moved, 0.0)
        if shift + high > LANE:
            out[at + 1] = out[at + 1] + jnp.where(lane < shift, moved, 0.0)
    return out


def scatter_lines(full, count, high):
    lane = lax.broadcasted_iota(jnp.int32, (8, LANE), 1)
    lines = []
    for i in range(count):
        at, shift = divmod(i * high, LANE)
        v = pltpu.roll(full[at], LANE - shift, axis=1) if shift else full[at]
        if shift + high > LANE:
            v = jnp.where(lane < LANE - shift, v, pltpu.roll(full[at + 1], LANE - shift, axis=1))
        lines.append(jnp.where(lane < high, v, 0.0))
    return lines


def prepare_kernel(*refs):
    sources, refs = refs[:9], refs[9:]
    (w_ref, z_ref, t_ref, vec_ref, xf_ref, cf_ref, db_ref), refs = refs[:7], refs[7:]
    r_ref, x_ref, c_ref, k_ref, *vec_refs, sem = refs
    copies = fetch(sources, (x_ref, c_ref, k_ref, *vec_refs, w_ref), sem)
    copies[2].wait()
    fill_taps(k_ref, r_ref, t_ref)
    for copy in copies[:2] + copies[3:]:
        copy.wait()
    rows, chans = xf_ref.shape
    for i, ref in enumerate(vec_refs):
        vec_ref[i : i + 1] = ref[...].reshape(1, chans)
    for i in range(4):
        split(x_ref[i].astype(F32), z_ref, i)
    xf_ref[...] = x_ref[...].astype(F32).reshape(rows, chans)
    cot = c_ref[...].astype(F32).reshape(rows, chans)
    cf_ref[...] = cot
    d_branch = cot * vec_ref[4:5]
    vec_ref[5:6] = jnp.sum(d_branch, axis=0, keepdims=True)
    vec_ref[6:8] = jnp.zeros((2, chans), F32)
    db_ref[...] = jnp.concatenate([d_branch, jnp.zeros((rows, 256 - chans), F32)], axis=1).astype(BF16)


def forward_kernel(last, me_ref, own_ref, p_ref, q_ref, t_ref, vec_ref, na_ref, unit_ref, s_ref, z_ref, u_ref, m_ref):
    fill_rim(last, me_ref, p_ref, q_ref, z_ref)
    z_ref[:, 3:7] = own_ref[...]
    stencil(z_ref, t_ref, s_ref, u_ref, False)

    def row(j, carry):
        main, rest = from_points(4, lambda u: u_ref[u, j])
        for i in range(4):
            at = pl.ds(pl.multiple_of(64 * i + 8 * j, 8), 8)
            m_ref[at, 0:LANE] = main[i]
            m_ref[at, LANE : LANE + 64] = rest[i][:, 0:64]
        return carry

    lax.fori_loop(0, 8, row, 0, unroll=8)
    chans = m_ref.shape[1]
    mixed = m_ref[...] + vec_ref[0:1]
    centred = mixed - jnp.mean(mixed, axis=-1, keepdims=True)
    inverse = lax.rsqrt(jnp.mean(centred * centred, axis=-1, keepdims=True) + 1e-06)
    unit = centred * inverse
    normed = unit * vec_ref[1:2] + vec_ref[2:3]
    rows = unit.shape[0]
    na_ref[:, 0:chans] = normed.astype(BF16)
    na_ref[:, chans:256] = jnp.zeros((rows, 256 - chans), BF16)
    unit_ref[:, 0:chans] = unit
    unit_ref[:, chans:256] = jnp.broadcast_to(inverse, (rows, 256 - chans))


def pointwise_kernel(me_ref, g0_ref, g1_ref, na_ref, unit_ref, xf_ref, cf_ref, db_ref, vec_ref, branch_ref, dm_ref, far_ref, w0_ref, w1_ref, small_ref, wi_ref, wo_ref, di_ref, do_ref, m_ref):
    rows, chans = xf_ref.shape
    normed = na_ref[...]
    d_b = db_ref[...]
    gamma = vec_ref[4:5]
    branch = jnp.zeros((rows, 256), F32)
    d_normed = jnp.zeros((rows, 256), F32)
    over_c = (((1,), (1,)), ((), ()))
    over_rows = (((0,), (0,)), ((), ()))
    pieces, high = g0_ref.shape[0], (g0_ref.shape[1] - 16) // 3
    low = low_lanes((high, LANE))
    first_row = lax.broadcasted_iota(jnp.int32, (16, LANE), 0) == 0
    lines, d_bias = [], []
    for i in range(2 * pieces):
        here = slice(i * high, i * high + high)
        g_ref, k = (g0_ref, i) if i < pieces else (g1_ref, i - pieces)
        rest = g_ref[k, high : 2 * high].astype(F32)
        wi_ref[here, 0:LANE] = g_ref[k, 0:high]
        wi_ref[here, LANE:256] = jnp.where(low, rest, 0.0).astype(BF16)
        wo_ref[here, 0:LANE] = g_ref[k, 2 * high : 3 * high]
        wo_ref[here, LANE:256] = jnp.where(low, pltpu.roll(rest, 64, axis=1), 0.0).astype(BF16)
        line = g_ref[k, 3 * high : 3 * high + 16].astype(F32)[0:1]
        lines.append(jnp.broadcast_to(line, (8, LANE)))
    bias = gather_lines(lines, high)
    total = 2 * pieces * high
    step = next(n for n in (768, 512, 256) if total % n == 0)
    for first in range(0, total, step):
        here = slice(first, first + step)
        w_in, w_out = wi_ref[here], wo_ref[here]
        line = jnp.concatenate([v[0:1] for v in bias[first // LANE : (first + step) // LANE]], axis=1)
        pre = lax.dot_general(normed, w_in, over_c, preferred_element_type=F32) + line
        d_hidden = lax.dot_general(d_b, w_out, over_c, preferred_element_type=F32)
        cdf = 0.5 * (1.0 + lax.erf(pre * root_half))
        hidden = (pre * cdf).astype(BF16)
        slope = cdf + pre * jnp.exp(-0.5 * pre * pre) * inv_root_tau
        d_pre = d_hidden * slope
        line = jnp.sum(d_pre, axis=0, keepdims=True)
        for at in range(0, step, LANE):
            d_bias.append(jnp.broadcast_to(line[:, at : at + LANE], (8, LANE)))
        d_pre = d_pre.astype(BF16)
        branch = branch + jnp.dot(hidden, w_out, preferred_element_type=F32)
        d_normed = d_normed + jnp.dot(d_pre, w_in, preferred_element_type=F32)
        di_ref[here] = lax.dot_general(d_pre, normed, over_rows, preferred_element_type=F32)
        do_ref[here] = lax.dot_general(hidden, d_b, over_rows, preferred_element_type=F32)
    for i, line in enumerate(scatter_lines(d_bias, 2 * pieces, high)):
        here = slice(i * high, i * high + high)
        w_ref, k = (w0_ref, i) if i < pieces else (w1_ref, i - pieces)
        rest = jnp.where(low, di_ref[here, LANE:256], pltpu.roll(do_ref[here, LANE:256], 64, axis=1))
        at = k * (3 * high + 16)
        w_ref[at : at + high] = di_ref[here, 0:LANE].astype(w_ref.dtype)
        w_ref[at + high : at + 2 * high] = rest.astype(w_ref.dtype)
        w_ref[at + 2 * high : at + 3 * high] = do_ref[here, 0:LANE].astype(w_ref.dtype)
        line = jnp.where(first_row, jnp.broadcast_to(line[0:1], (16, LANE)), 0.0)
        w_ref[at + 3 * high : at + 3 * high + 16] = line.astype(w_ref.dtype)
    branch = branch[:, 0:chans] + vec_ref[3:4]
    branch_ref[...] = gamma * branch
    d_normed = d_normed[:, 0:chans]
    unit = unit_ref[:, 0:chans]
    inverse = unit_ref[:, chans : chans + 1]
    scaled = d_normed * vec_ref[1:2]
    d_mixed = inverse * (
        scaled
        - jnp.mean(scaled, axis=-1, keepdims=True)
        - unit * jnp.mean(scaled * unit, axis=-1, keepdims=True)
    )
    dm_ref[...] = d_mixed.reshape(dm_ref.shape).astype(BF16)
    m_ref[...] = d_mixed.reshape(m_ref.shape)
    odd = lax.rem(me_ref[0], 2)
    pack_planes(1 - odd, lambda i: m_ref[i], w1_ref, w0_ref.shape[0])
    pack_planes(odd, lambda i: m_ref[i], far_ref)
    small_ref[...] = jnp.zeros(small_ref.shape, F32)
    sums = (d_mixed, d_normed * unit, d_normed, None, cf_ref[...] * branch)
    for i, term in enumerate(sums):
        total = vec_ref[5:6] if term is None else jnp.sum(term, axis=0, keepdims=True)
        small_ref[i : i + 1, 0:chans] = total


def rows_to_one(v, p_ref):
    for b, x in enumerate(v):
        p_ref[8 * b : 8 * b + 8] = x
    total = p_ref[pl.ds(0, 8, stride=8), :]
    for k in range(1, 8):
        total = total + p_ref[pl.ds(k, 8, stride=8), :]
    return total


HALF = 272


def block(g):
    return 64 * (g // 7) + 8 * (g % 7)


def main_at(g):
    return (0, 7 * g) if g < 38 else (1, 7 * (g - 38))


def rest_at(g):
    return 77 + 7 * (g % 25), 64 * (g // 25)


def grad_kernel(me_ref, s_ref, g_ref, small_ref, keep_ref, send_ref, z_ref, t_ref, o_ref, wa_ref, wb_ref, w_ref, p_ref):
    p_ref[:, 56:64] = jnp.zeros((7, 8, LANE), F32)
    odd = lax.rem(me_ref[0], 2)
    for i in range(4):
        split(g_ref[i].astype(F32), z_ref, i)

    def row(j, carry):
        def store(u, v):
            t_ref[u, j] = v

        to_points(evaluation(4), lambda k: z_ref[0, k, j], lambda k: z_ref[1, k, j], store)
        return carry

    lax.fori_loop(0, 8, row, 0, unroll=8)

    def unit(u, carry):
        grads = [t_ref[u, j] for j in range(8)]
        for e in range(7):
            acc = [None] * 7
            for source in range(8):
                x = s_ref[e, u, source]
                for b in range(7):
                    j = source - b + 3
                    if 0 <= j < 8:
                        term = x * grads[j]
                        acc[b] = term if acc[b] is None else acc[b] + term
            o_ref[u, e] = rows_to_one(acc, p_ref.at[e])
        return carry

    lax.fori_loop(0, 3 * (PAIRS + 1), unit, 0, unroll=3)

    for e in range(7):
        main, rest = from_points(7, lambda u: o_ref[u, e])
        for a in range(7):
            wa_ref[pl.ds(a * 64 + e, 8, stride=8), :] = main[a]
            one = jnp.where(low_lanes((8, LANE)), rest[a], pltpu.roll(rest[a], 64, axis=1))
            wb_ref[pl.ds(a * 64 + e, 8, stride=8), :] = one

    w_ref[0, HALF - 16 : HALF] = jnp.zeros((16, LANE), F32)
    w_ref[1, HALF - 16 : HALF] = jnp.zeros((16, LANE), F32)
    low = low_lanes((8, LANE))[0:7]
    for g in range(49):
        half, row = main_at(g)
        w_ref[half, row : row + 7] = wa_ref[block(g) : block(g) + 7]
        row, lane = rest_at(g)
        if lane == 0:
            pair = min(g + 25, 48)
            w_ref[1, row : row + 7] = jnp.where(
                low, wb_ref[block(g) : block(g) + 7], wb_ref[block(pair) : block(pair) + 7]
            )
    w_ref[0, 266:271] = small_ref[0:5, 0:LANE]
    w_ref[1, 252:257] = small_ref[0:5, LANE:256]
    keep_ref[...] = w_ref[odd]
    send_ref[...] = w_ref[1 - odd].astype(BF16)


def final_kernel(scale, me_ref, mine_ref, other_ref, total_ref, dk_ref, *refs):
    odd, small_refs, (wi_ref, bi_ref, wo_ref, w_ref) = lax.rem(me_ref[0], 2), refs[:5], refs[5:]
    total = total_ref[...] * scale
    units = wi_ref.shape[0]
    high = (total.shape[0] - 16) // 3
    rest = total[high : high + units]
    wi_ref[:, 0:LANE] = total[0:units]
    wi_ref[:, LANE : LANE + 64] = rest[:, 0:64]
    wo_ref[:, 0:LANE] = total[2 * high : 2 * high + units]
    wo_ref[:, LANE : LANE + 64] = rest[:, 64:LANE]
    bi_ref[...] = total[3 * high : 3 * high + 1, 0:units]
    w_ref[odd] = mine_ref[...].astype(F32) * scale
    w_ref[1 - odd] = other_ref[...].astype(F32) * scale
    for g in range(49):
        half, row = main_at(g)
        dk_ref[g // 7, g % 7, :, 0:LANE] = w_ref[half, row : row + 7]
        row, lane = rest_at(g)
        dk_ref[g // 7, g % 7, :, LANE : LANE + 64] = w_ref[1, row : row + 7][:, lane : lane + 64]
    for i, ref in enumerate(small_refs):
        ref[:, 0:LANE] = w_ref[0, 266 + i : 267 + i]
        ref[:, LANE : LANE + 64] = w_ref[1, 252 + i : 253 + i, 0:64]


def back_kernel(last, me_ref, g_ref, p_ref, q_ref, t_ref, c_ref, xf_ref, branch_ref, dx_ref, out_ref, z_ref, s_ref, u_ref):
    fill_rim(last, me_ref, p_ref, q_ref, z_ref)
    for i in range(4):
        split(g_ref[i].astype(F32), z_ref, 3 + i)
    out_ref[...] = (xf_ref[...] + branch_ref[...]).reshape(out_ref.shape).astype(BF16)
    stencil(z_ref, t_ref, s_ref, u_ref, True)
    main, rest = from_points(4, lambda u: u_ref[u], 6)
    for i in range(4):
        cot = c_ref[64 * i : 64 * i + 64].reshape(8, 8, c_ref.shape[1])
        dx_ref[i, :, :, 0:LANE] = (cot[:, :, 0:LANE] + main[i]).astype(BF16)
        dx_ref[i, :, :, LANE : LANE + 64] = (cot[:, :, LANE:] + rest[i][:, :, 0:64]).astype(BF16)


def params(mib):
    return pltpu.CompilerParams(vmem_limit_bytes=mib * 1024 * 1024)


def cost(us):
    return pl.CostEstimate(flops=int(us * 1.0e9), bytes_accessed=0, transcendentals=0)


def struct(shape, dtype):
    return jax.ShapeDtypeStruct(shape, dtype)


def on_device(
    features, cotangent, kernel, b_dw, ln_gain, ln_bias, w_in_t, b_in, w_out, b_out, gamma
):
    size_x, size_y, size_z, chans = features.shape
    devices = lax.axis_size("space")
    scale = float(size_x * devices * size_y * size_z) ** (-0.5)
    rows = size_x * size_y * size_z
    units = w_in_t.shape[0]
    bits = [1 << i for i in range(devices.bit_length() - 1)]
    order, sums_order = bits, [bits[0], bits[-1], bits[1]] + bits[2:-1]
    me = lax.axis_index("space").astype(jnp.int32).reshape(1)
    def call(body, name, us, mib, out_shape, operands, scratch=(), spec=VMEM):
        specs = [SMEM if x is me else spec for x in operands]
        return pl.pallas_call(
            body,
            out_shape=out_shape,
            in_specs=specs,
            out_specs=jax.tree.map(lambda _: VMEM, out_shape),
            scratch_shapes=list(scratch),
            compiler_params=params(mib),
            name=name,
            cost_estimate=cost(us),
        )(*operands)

    z_scratch = pltpu.VMEM((2, 10, size_y, size_z, LANE), F32)
    u_scratch = pltpu.VMEM((15, size_y, size_z, LANE), F32)
    shifts = (7, 15, size_y, size_z, LANE)
    cells = struct((rows, chans), F32)

    high = -(-units // 16) * 16
    lines = 3 * high + 16
    rim = struct((3 * size_y * size_z * 3 // 2, LANE), BF16)
    raw = (w_in_t, b_in, w_out, features)
    piece, to_core, to_far = call(
        pack_kernel,
        "pack",
        1.0,
        56,
        (struct((lines, LANE), BF16), rim, rim),
        (me,) + raw,
        [pltpu.VMEM(x.shape, x.dtype) for x in raw] + [pltpu.SemaphoreType.DMA((4,))],
        HBM,
    )
    x_core, x_far = swap(to_core, 1), swap_odd(to_far)
    weights = swap(piece, order[-1])
    given = (features, cotangent, kernel, b_dw, ln_gain, ln_bias, b_out, gamma, piece)
    prepared = call(
        prepare_kernel,
        "prepare",
        1.0,
        6,
        (
            struct((lines, LANE), BF16),
            struct((2, 4, size_y, size_z, LANE), F32),
            struct((16, 7, 8, LANE), F32),
            struct((8, chans), F32),
            cells,
            cells,
            struct((rows, 256), BF16),
        ),
        given,
        [pltpu.VMEM((2, 7, 7, 8, LANE), F32)]
        + [pltpu.VMEM(x.shape, x.dtype) for x in given[:-1]]
        + [pltpu.SemaphoreType.DMA((len(given),))],
        HBM,
    )
    weights, x_core, prepared = lax.optimization_barrier((weights, x_core, prepared))
    piece, own, taps, vecs, x_f32, cot_f32, d_branch = prepared
    weights = jnp.stack([piece, weights])
    for bit in order[-2:2:-1]:
        weights = jnp.concatenate([weights, swap(weights, bit)], axis=0)
    over_z, over_x = swap(weights, order[2]), swap(weights, order[1])
    over_z, over_x, x_far = lax.optimization_barrier((over_z, over_x, x_far))
    n = over_z.shape[0] // 2
    corner = swap(over_z[:n], order[1]), swap(over_x[n:], order[2])
    weights = jnp.concatenate([weights, over_z, over_x, *corner], axis=0)
    forward = call(
        functools.partial(forward_kernel, devices - 1),
        "forward_stencil",
        2.5,
        10,
        (struct((rows, 256), BF16), struct((rows, 256), F32), struct(shifts, F32)),
        (me, own, x_core, x_far, taps, vecs),
        [z_scratch, u_scratch, pltpu.VMEM((rows, chans), F32)],
    )
    weights, forward = lax.optimization_barrier((weights, forward))
    normed, unit, shifted_x = forward
    weights_other = swap(weights, 1)

    pieces = weights.shape[0]
    branch, d_mixed, to_far, grad_keep, to_core, small = call(
        pointwise_kernel,
        "pointwise",
        2.5,
        16,
        (
            cells,
            struct(features.shape, BF16),
            rim,
            struct((pieces * lines, LANE), F32),
            struct((pieces * lines + rim.shape[0], LANE), BF16),
            struct((8, 256), F32),
        ),
        (me, weights, weights_other, normed, unit, x_f32, cot_f32, d_branch, vecs),
        [pltpu.VMEM((2 * pieces * high, 256), BF16)] * 2
        + [pltpu.VMEM((2 * pieces * high, 256), F32)] * 2
        + [pltpu.VMEM((size_x, size_y * size_z, chans), F32)],
    )
    keep, send = call(
        grad_kernel,
        "kernel_gradient",
        2.0,
        10,
        (struct((HALF, LANE), F32), struct((HALF, LANE), BF16)),
        (me, shifted_x, d_mixed, small),
        [
            pltpu.VMEM((2, 4, size_y, size_z, LANE), F32),
            u_scratch,
            pltpu.VMEM((15, 7, 8, LANE), F32),
            pltpu.VMEM((448, LANE), F32),
            pltpu.VMEM((448, LANE), F32),
            pltpu.VMEM((2, HALF, LANE), F32),
            pltpu.VMEM((7, 64, LANE), F32),
        ],
    )

    from_core = swap(to_core, 1)
    total = grad_keep + from_core[: pieces * lines].astype(F32)
    g_core = from_core[pieces * lines :]
    send, to_far = lax.optimization_barrier((send, to_far))
    sums = keep + swap(send, 1).astype(F32)
    g_far = swap_odd(to_far)
    for step, (bit, sums_bit) in enumerate(zip(order[1:], sums_order[1:])):
        n = total.shape[0] // 2
        mine, kept = sums.astype(BF16), total[:n]
        theirs = swap(mine, sums_bit)
        got = swap(total[n:].astype(BF16), bit)
        if step == 0:
            theirs, g_far = lax.optimization_barrier((theirs, g_far))
        if step == len(order) - 3:
            d_x, output = call(
                functools.partial(back_kernel, devices - 1),
                "backward_stencil",
                2.5,
                10,
                (struct(features.shape, BF16),) * 2,
                (me, d_mixed, g_core, g_far, taps, cot_f32, x_f32, branch),
                [z_scratch, pltpu.VMEM(shifts, F32), u_scratch],
            )
            theirs, d_x, output = lax.optimization_barrier((theirs, d_x, output))
        if step < len(order) - 2:
            theirs, got = lax.optimization_barrier((theirs, got))
        sums = mine.astype(F32) + theirs.astype(F32)
        total = kept + got.astype(F32)
    mine = sums.astype(BF16)
    other = swap(mine, 1)
    total = lax.optimization_barrier(kept + got.astype(F32))
    d_kernel, *vectors, d_w_in, d_b_in, d_w_out = call(
        functools.partial(final_kernel, scale),
        "final",
        1.0,
        4,
        (struct(kernel.shape, F32),)
        + (struct((1, chans), F32),) * 5
        + (struct((units, chans), F32), struct((1, units), F32), struct((units, chans), F32)),
        (me, mine, other, total),
        [pltpu.VMEM((2, HALF, LANE), F32)],
    )
    d_b_dw, d_ln_gain, d_ln_bias, d_b_out, d_gamma = [v.reshape(chans) for v in vectors]
    return (
        output,
        d_x,
        d_kernel,
        d_b_dw,
        d_ln_gain,
        d_ln_bias,
        d_w_in,
        d_b_in.reshape(units),
        d_w_out,
        d_b_out,
        d_gamma,
    )


def solution(mesh):
    in_specs = (
        P(("crop", "space"), None, None, None),
        P(("crop", "space"), None, None, None),
        P(),
        P(),
        P(),
        P(),
        P("space", None),
        P("space"),
        P("space", None),
        P(),
        P(),
    )
    out_specs = (
        P(("crop", "space"), None, None, None),
        P(("crop", "space"), None, None, None),
        P("crop", None, None, None),
        P("crop"),
        P("crop"),
        P("crop"),
        P(("crop", "space"), None),
        P(("crop", "space")),
        P(("crop", "space"), None),
        P("crop"),
        P("crop"),
    )
    return jax.shard_map(
        on_device, mesh=mesh, in_specs=in_specs, out_specs=out_specs, check_vma=False
    )
```

```python
import functools

import jax
import jax.numpy as jnp
import numpy as np
from jax import lax
from jax.experimental import pallas as pl
from jax.experimental.pallas import tpu as pltpu
from jax.sharding import PartitionSpec as P

root_half = 0.7071067811865476
inv_root_tau = 0.3989422804014327
F32 = jnp.float32
BF16 = jnp.bfloat16
LANE = 128
VMEM = pl.BlockSpec(memory_space=pltpu.VMEM)
HBM = pl.BlockSpec(memory_space=pltpu.HBM)
SMEM = pl.BlockSpec(memory_space=pltpu.SMEM)

POINTS = (0.4, 0.8, 1.25, 2.5)
PAIRS = len(POINTS)


def analysis():
    finite = [0.0] + [sign * p for p in POINTS for sign in (1.0, -1.0)]
    vander = np.array([[x**k for k in range(10)] for x in finite] + [[0.0] * 9 + [1.0]])
    inverse = np.linalg.inv(vander).T
    even = [{k: float(inverse[1 + 2 * q, k]) for k in (2, 4, 6, 8)} for q in range(PAIRS)]
    odd = [{k: float(inverse[1 + 2 * q, k]) for k in (1, 3, 5, 7)} for q in range(PAIRS)]
    zero = {k: float(inverse[0, k]) for k in (0, 2, 4, 6, 8)}
    infinity = {k: float(inverse[9, k]) for k in (1, 3, 5, 7, 9)}
    return even, odd, zero, infinity


def evaluation(size):
    even = [{k: p**k for k in range(0, size, 2)} for p in POINTS]
    odd = [{k: p**k for k in range(1, size, 2)} for p in POINTS]
    return even, odd, {0: 1.0}, {size - 1: 1.0}


def weighted(load, weights):
    total = None
    for k, w in weights.items():
        term = load(k) if w == 1.0 else load(k) * w
        total = term if total is None else total + term
    return total


def low_lanes(shape):
    return lax.broadcasted_iota(jnp.int32, shape, len(shape) - 1) < 64


def to_points(tables, main, rest, store):
    even, odd, zero, infinity = tables
    for q in range(PAIRS):
        e, o = weighted(main, even[q]), weighted(main, odd[q])
        store(1 + 2 * q, e + o)
        store(2 + 2 * q, e - o)
        e, o = weighted(rest, even[q]), weighted(rest, odd[q])
        store(10 + q, jnp.where(low_lanes(e.shape), e + o, e - o))
    store(0, weighted(main, zero))
    store(9, weighted(main, infinity))
    z, i = weighted(rest, zero), weighted(rest, infinity)
    store(14, jnp.where(low_lanes(z.shape), z, i))


def from_points(size, load, power=0):
    main, rest = [None] * size, [None] * size

    def add(into, k, v, w):
        term = v if w == 1.0 else v * w
        into[k] = term if into[k] is None else into[k] + term

    for q in range(PAIRS):
        plus, minus, both = load(1 + 2 * q), load(2 + 2 * q), load(10 + q)
        swapped = pltpu.roll(both, 64, axis=both.ndim - 1)
        sums = (plus + minus, both + swapped), (plus - minus, both - swapped)
        for k in range(size):
            m, r = sums[k % 2]
            add(main, k, m, POINTS[q] ** (k + power))
            add(rest, k, r, POINTS[q] ** (k + power))
    ends = load(14)
    add(main, 0, load(0), 1.0)
    add(rest, 0, ends, 1.0)
    add(main, size - 1, load(9), 1.0)
    add(rest, size - 1, pltpu.roll(ends, 64, axis=ends.ndim - 1), 1.0)
    return main, rest


def swap(x, bit):
    size = lax.axis_size("space")
    return lax.ppermute(x, "space", [(i, i ^ bit) for i in range(size)])


def swap_odd(x):
    size = lax.axis_size("space")
    return lax.ppermute(x, "space", [(i, (i + 1 if i % 2 else i - 1) % size) for i in range(size)])


def shifted(v, by):
    if by == 0:
        return v
    row = lax.broadcasted_iota(jnp.int32, v.shape, 0)
    keep = (row < 8 - by) if by > 0 else (row >= -by)
    return jnp.where(keep, pltpu.roll(v, (-by) % 8, axis=0), 0.0)


def split(v, z_ref, plane):
    z_ref[0, plane] = v[..., :LANE]
    z_ref[1, plane, ..., 0:64] = v[..., LANE:]
    z_ref[1, plane, ..., 64:128] = v[..., LANE:]


def pack_planes(first, load, out_ref, base=0):
    for k in range(3):
        v = load(first + k)
        cells = v.shape[0]
        at = base + k * cells * 3 // 2
        out_ref[at : at + cells] = v[:, :LANE].astype(BF16)
        pair = jnp.concatenate([v[: cells // 2, LANE:], v[cells // 2 :, LANE:]], axis=1)
        out_ref[at + cells : at + cells * 3 // 2] = pair.astype(BF16)


def fill_rim(last, me_ref, p_ref, q_ref, z_ref):
    me = me_ref[0]
    odd = lax.rem(me, 2) == 1
    p, q = p_ref[...].astype(F32), q_ref[...].astype(F32)
    before = jnp.where(me == 0, 0.0, jnp.where(odd, p, q))
    after = jnp.where(me == last, 0.0, jnp.where(odd, q, p))
    rows, cols = z_ref.shape[2], z_ref.shape[3]
    cells = rows * cols
    for k in range(3):
        at = k * cells * 3 // 2
        for v, plane in ((before, k), (after, k + 7)):
            z_ref[0, plane] = v[at : at + cells].reshape(rows, cols, LANE)
            pair = v[at + cells : at + cells * 3 // 2]
            swapped = pltpu.roll(pair, 64, axis=1)
            low = low_lanes(pair.shape)
            z_ref[1, plane, : rows // 2] = jnp.where(low, pair, swapped).reshape(rows // 2, cols, LANE)
            z_ref[1, plane, rows // 2 :] = jnp.where(low, swapped, pair).reshape(rows // 2, cols, LANE)


def fill_taps(k_ref, r_ref, t_ref):
    for a in range(7):
        for b in range(7):
            v = k_ref[a, b]
            r_ref[0, a, b, 0:7] = v[:, :LANE]
            r_ref[1, a, b, 0:7, 0:64] = v[:, LANE:]
            r_ref[1, a, b, 0:7, 64:128] = v[:, LANE:]
    for b in range(7):

        def store(u, v):
            t_ref[u, b] = v
            if u == 14:
                t_ref[15, b] = pltpu.roll(v, 64, axis=1)

        to_points(evaluation(7), lambda k: r_ref[0, k, b], lambda k: r_ref[1, k, b], store)


def reversed_unit(u):
    same_sign = 2 * PAIRS - 1 - 2 * ((u - 1) // 2) + (u - 1) % 2
    paired = 19 + PAIRS - u
    return jnp.where(
        u == 0, 9, jnp.where(u < 9, same_sign, jnp.where(u == 9, 0, jnp.where(u < 14, paired, 15)))
    )


def stencil(z_ref, t_ref, s_ref, u_ref, flip):
    def row(j, carry):
        def store(u, v):
            s_ref[3, u, j] = v

        to_points(analysis(), lambda k: z_ref[0, k, j], lambda k: z_ref[1, k, j], store)
        return carry

    lax.fori_loop(0, 8, row, 0, unroll=8)

    def unit(u, carry):
        taps_at = reversed_unit(u) if flip else u
        rows = [s_ref[3, u, j] for j in range(8)]
        for e in range(7):
            if e != 3:
                for j in range(8):
                    s_ref[e, u, j] = shifted(rows[j], e - 3)
        acc = [None] * 8
        for e in range(7):
            taps = []
            for b in range(7):
                fb, fe = (6 - b, 6 - e) if flip else (b, e)
                taps.append(jnp.broadcast_to(t_ref[taps_at, fb, fe : fe + 1], (8, LANE)))
            for source in range(8):
                x = rows[source] if e == 3 else s_ref[e, u, source]
                for b in range(7):
                    j = source - b + 3
                    if 0 <= j < 8:
                        term = x * taps[b]
                        acc[j] = term if acc[j] is None else acc[j] + term
        for j in range(8):
            u_ref[u, j] = acc[j]
        return carry

    lax.fori_loop(0, 3 * (PAIRS + 1), unit, 0, unroll=3)


def fetch(sources, targets, sem):
    copies = [pltpu.make_async_copy(x, y, sem.at[i]) for i, (x, y) in enumerate(zip(sources, targets))]
    for copy in copies:
        copy.start()
    return copies


def pack_kernel(me_ref, wi_hbm, b_hbm, wo_hbm, x_hbm, out_ref, core_ref, far_ref, wi_ref, b_ref, wo_ref, x_ref, sem):
    copies = fetch((x_hbm, wi_hbm, b_hbm, wo_hbm), (x_ref, wi_ref, b_ref, wo_ref), sem)
    units = wi_ref.shape[0]
    high = (out_ref.shape[0] - 16) // 3
    out_ref[...] = jnp.zeros(out_ref.shape, BF16)
    for copy in copies:
        copy.wait()
    w_in, w_out = wi_ref[...].astype(F32), wo_ref[...].astype(F32)
    out_ref[0:units] = w_in[:, :LANE].astype(BF16)
    out_ref[high : high + units] = jnp.concatenate([w_in[:, LANE:], w_out[:, LANE:]], axis=1).astype(BF16)
    out_ref[2 * high : 2 * high + units] = w_out[:, :LANE].astype(BF16)
    line = b_ref[...].astype(F32).reshape(1, units)
    line = jnp.concatenate([line, jnp.zeros((1, LANE - units), F32)], axis=1)
    first = lax.broadcasted_iota(jnp.int32, (16, LANE), 0) == 0
    out_ref[3 * high : 3 * high + 16] = jnp.where(first, jnp.broadcast_to(line, (16, LANE)), 0.0).astype(BF16)
    odd = lax.rem(me_ref[0], 2)

    def plane(i):
        v = x_ref[i].astype(F32)
        return v.reshape(v.shape[0] * v.shape[1], v.shape[2])

    pack_planes(1 - odd, plane, core_ref)
    pack_planes(odd, plane, far_ref)


def gather_lines(lines, high):
    count = -(-len(lines) * high // LANE)
    out = [jnp.zeros((8, LANE), F32)] * count
    lane = lax.broadcasted_iota(jnp.int32, (8, LANE), 1)
    for i, line in enumerate(lines):
        at, shift = divmod(i * high, LANE)
        moved = pltpu.roll(line, shift, axis=1) if shift else line
        out[at] = out[at] + jnp.where(lane >= shift, moved, 0.0)
        if shift + high > LANE:
            out[at + 1] = out[at + 1] + jnp.where(lane < shift, moved, 0.0)
    return out


def scatter_lines(full, count, high):
    lane = lax.broadcasted_iota(jnp.int32, (8, LANE), 1)
    lines = []
    for i in range(count):
        at, shift = divmod(i * high, LANE)
        v = pltpu.roll(full[at], LANE - shift, axis=1) if shift else full[at]
        if shift + high > LANE:
            v = jnp.where(lane < LANE - shift, v, pltpu.roll(full[at + 1], LANE - shift, axis=1))
        lines.append(jnp.where(lane < high, v, 0.0))
    return lines


def prepare_kernel(*refs):
    sources, refs = refs[:9], refs[9:]
    (w_ref, z_ref, t_ref, vec_ref, xf_ref, cf_ref, db_ref), refs = refs[:7], refs[7:]
    r_ref, x_ref, c_ref, k_ref, *vec_refs, sem = refs
    copies = fetch(sources, (x_ref, c_ref, k_ref, *vec_refs, w_ref), sem)
    copies[2].wait()
    fill_taps(k_ref, r_ref, t_ref)
    for copy in copies[:2] + copies[3:]:
        copy.wait()
    rows, chans = xf_ref.shape
    for i, ref in enumerate(vec_refs):
        vec_ref[i : i + 1] = ref[...].reshape(1, chans)
    for i in range(4):
        split(x_ref[i].astype(F32), z_ref, i)
    xf_ref[...] = x_ref[...].astype(F32).reshape(rows, chans)
    cot = c_ref[...].astype(F32).reshape(rows, chans)
    cf_ref[...] = cot
    d_branch = cot * vec_ref[4:5]
    vec_ref[5:6] = jnp.sum(d_branch, axis=0, keepdims=True)
    vec_ref[6:8] = jnp.zeros((2, chans), F32)
    db_ref[...] = jnp.concatenate([d_branch, jnp.zeros((rows, 256 - chans), F32)], axis=1).astype(BF16)


def forward_kernel(last, me_ref, own_ref, p_ref, q_ref, t_ref, vec_ref, na_ref, unit_ref, s_ref, z_ref, u_ref, m_ref):
    fill_rim(last, me_ref, p_ref, q_ref, z_ref)
    z_ref[:, 3:7] = own_ref[...]
    stencil(z_ref, t_ref, s_ref, u_ref, False)

    def row(j, carry):
        main, rest = from_points(4, lambda u: u_ref[u, j])
        for i in range(4):
            at = pl.ds(pl.multiple_of(64 * i + 8 * j, 8), 8)
            m_ref[at, 0:LANE] = main[i]
            m_ref[at, LANE : LANE + 64] = rest[i][:, 0:64]
        return carry

    lax.fori_loop(0, 8, row, 0, unroll=8)
    chans = m_ref.shape[1]
    mixed = m_ref[...] + vec_ref[0:1]
    centred = mixed - jnp.mean(mixed, axis=-1, keepdims=True)
    inverse = lax.rsqrt(jnp.mean(centred * centred, axis=-1, keepdims=True) + 1e-06)
    unit = centred * inverse
    normed = unit * vec_ref[1:2] + vec_ref[2:3]
    rows = unit.shape[0]
    na_ref[:, 0:chans] = normed.astype(BF16)
    na_ref[:, chans:256] = jnp.zeros((rows, 256 - chans), BF16)
    unit_ref[:, 0:chans] = unit
    unit_ref[:, chans:256] = jnp.broadcast_to(inverse, (rows, 256 - chans))


def pointwise_kernel(me_ref, g0_ref, g1_ref, na_ref, unit_ref, xf_ref, cf_ref, db_ref, vec_ref, branch_ref, dm_ref, far_ref, w0_ref, w1_ref, small_ref, wi_ref, wo_ref, di_ref, do_ref, m_ref):
    rows, chans = xf_ref.shape
    normed = na_ref[...]
    d_b = db_ref[...]
    gamma = vec_ref[4:5]
    branch = jnp.zeros((rows, 256), F32)
    d_normed = jnp.zeros((rows, 256), F32)
    over_c = (((1,), (1,)), ((), ()))
    over_rows = (((0,), (0,)), ((), ()))
    pieces, high = g0_ref.shape[0], (g0_ref.shape[1] - 16) // 3
    low = low_lanes((high, LANE))
    first_row = lax.broadcasted_iota(jnp.int32, (16, LANE), 0) == 0
    lines, d_bias = [], []
    for i in range(2 * pieces):
        here = slice(i * high, i * high + high)
        g_ref, k = (g0_ref, i) if i < pieces else (g1_ref, i - pieces)
        rest = g_ref[k, high : 2 * high].astype(F32)
        wi_ref[here, 0:LANE] = g_ref[k, 0:high]
        wi_ref[here, LANE:256] = jnp.where(low, rest, 0.0).astype(BF16)
        wo_ref[here, 0:LANE] = g_ref[k, 2 * high : 3 * high]
        wo_ref[here, LANE:256] = jnp.where(low, pltpu.roll(rest, 64, axis=1), 0.0).astype(BF16)
        line = g_ref[k, 3 * high : 3 * high + 16].astype(F32)[0:1]
        lines.append(jnp.broadcast_to(line, (8, LANE)))
    bias = gather_lines(lines, high)
    total = 2 * pieces * high
    step = next(n for n in (768, 512, 256) if total % n == 0)
    for first in range(0, total, step):
        here = slice(first, first + step)
        w_in, w_out = wi_ref[here], wo_ref[here]
        line = jnp.concatenate([v[0:1] for v in bias[first // LANE : (first + step) // LANE]], axis=1)
        pre = lax.dot_general(normed, w_in, over_c, preferred_element_type=F32) + line
        d_hidden = lax.dot_general(d_b, w_out, over_c, preferred_element_type=F32)
        cdf = 0.5 * (1.0 + lax.erf(pre * root_half))
        hidden = (pre * cdf).astype(BF16)
        slope = cdf + pre * jnp.exp(-0.5 * pre * pre) * inv_root_tau
        d_pre = d_hidden * slope
        line = jnp.sum(d_pre, axis=0, keepdims=True)
        for at in range(0, step, LANE):
            d_bias.append(jnp.broadcast_to(line[:, at : at + LANE], (8, LANE)))
        d_pre = d_pre.astype(BF16)
        branch = branch + jnp.dot(hidden, w_out, preferred_element_type=F32)
        d_normed = d_normed + jnp.dot(d_pre, w_in, preferred_element_type=F32)
        di_ref[here] = lax.dot_general(d_pre, normed, over_rows, preferred_element_type=F32)
        do_ref[here] = lax.dot_general(hidden, d_b, over_rows, preferred_element_type=F32)
    for i, line in enumerate(scatter_lines(d_bias, 2 * pieces, high)):
        here = slice(i * high, i * high + high)
        w_ref, k = (w0_ref, i) if i < pieces else (w1_ref, i - pieces)
        rest = jnp.where(low, di_ref[here, LANE:256], pltpu.roll(do_ref[here, LANE:256], 64, axis=1))
        at = k * (3 * high + 16)
        w_ref[at : at + high] = di_ref[here, 0:LANE].astype(w_ref.dtype)
        w_ref[at + high : at + 2 * high] = rest.astype(w_ref.dtype)
        w_ref[at + 2 * high : at + 3 * high] = do_ref[here, 0:LANE].astype(w_ref.dtype)
        line = jnp.where(first_row, jnp.broadcast_to(line[0:1], (16, LANE)), 0.0)
        w_ref[at + 3 * high : at + 3 * high + 16] = line.astype(w_ref.dtype)
    branch = branch[:, 0:chans] + vec_ref[3:4]
    branch_ref[...] = gamma * branch
    d_normed = d_normed[:, 0:chans]
    unit = unit_ref[:, 0:chans]
    inverse = unit_ref[:, chans : chans + 1]
    scaled = d_normed * vec_ref[1:2]
    d_mixed = inverse * (
        scaled
        - jnp.mean(scaled, axis=-1, keepdims=True)
        - unit * jnp.mean(scaled * unit, axis=-1, keepdims=True)
    )
    dm_ref[...] = d_mixed.reshape(dm_ref.shape).astype(BF16)
    m_ref[...] = d_mixed.reshape(m_ref.shape)
    odd = lax.rem(me_ref[0], 2)
    pack_planes(1 - odd, lambda i: m_ref[i], w1_ref, w0_ref.shape[0])
    pack_planes(odd, lambda i: m_ref[i], far_ref)
    small_ref[...] = jnp.zeros(small_ref.shape, F32)
    sums = (d_mixed, d_normed * unit, d_normed, None, cf_ref[...] * branch)
    for i, term in enumerate(sums):
        total = vec_ref[5:6] if term is None else jnp.sum(term, axis=0, keepdims=True)
        small_ref[i : i + 1, 0:chans] = total


def rows_to_one(v, p_ref):
    for b, x in enumerate(v):
        p_ref[8 * b : 8 * b + 8] = x
    total = p_ref[pl.ds(0, 8, stride=8), :]
    for k in range(1, 8):
        total = total + p_ref[pl.ds(k, 8, stride=8), :]
    return total


HALF = 272


def block(g):
    return 64 * (g // 7) + 8 * (g % 7)


def main_at(g):
    return (0, 7 * g) if g < 38 else (1, 7 * (g - 38))


def rest_at(g):
    return 77 + 7 * (g % 25), 64 * (g // 25)


def grad_kernel(me_ref, s_ref, g_ref, small_ref, keep_ref, send_ref, z_ref, t_ref, o_ref, wa_ref, wb_ref, w_ref, p_ref):
    p_ref[:, 56:64] = jnp.zeros((7, 8, LANE), F32)
    odd = lax.rem(me_ref[0], 2)
    for i in range(4):
        split(g_ref[i].astype(F32), z_ref, i)

    def row(j, carry):
        def store(u, v):
            t_ref[u, j] = v

        to_points(evaluation(4), lambda k: z_ref[0, k, j], lambda k: z_ref[1, k, j], store)
        return carry

    lax.fori_loop(0, 8, row, 0, unroll=8)

    def unit(u, carry):
        grads = [t_ref[u, j] for j in range(8)]
        for e in range(7):
            acc = [None] * 7
            for source in range(8):
                x = s_ref[e, u, source]
                for b in range(7):
                    j = source - b + 3
                    if 0 <= j < 8:
                        term = x * grads[j]
                        acc[b] = term if acc[b] is None else acc[b] + term
            o_ref[u, e] = rows_to_one(acc, p_ref.at[e])
        return carry

    lax.fori_loop(0, 3 * (PAIRS + 1), unit, 0, unroll=3)

    for e in range(7):
        main, rest = from_points(7, lambda u: o_ref[u, e])
        for a in range(7):
            wa_ref[pl.ds(a * 64 + e, 8, stride=8), :] = main[a]
            one = jnp.where(low_lanes((8, LANE)), rest[a], pltpu.roll(rest[a], 64, axis=1))
            wb_ref[pl.ds(a * 64 + e, 8, stride=8), :] = one

    w_ref[0, HALF - 16 : HALF] = jnp.zeros((16, LANE), F32)
    w_ref[1, HALF - 16 : HALF] = jnp.zeros((16, LANE), F32)
    low = low_lanes((8, LANE))[0:7]
    for g in range(49):
        half, row = main_at(g)
        w_ref[half, row : row + 7] = wa_ref[block(g) : block(g) + 7]
        row, lane = rest_at(g)
        if lane == 0:
            pair = min(g + 25, 48)
            w_ref[1, row : row + 7] = jnp.where(
                low, wb_ref[block(g) : block(g) + 7], wb_ref[block(pair) : block(pair) + 7]
            )
    w_ref[0, 266:271] = small_ref[0:5, 0:LANE]
    w_ref[1, 252:257] = small_ref[0:5, LANE:256]
    keep_ref[...] = w_ref[odd]
    send_ref[...] = w_ref[1 - odd].astype(BF16)


def final_kernel(scale, me_ref, mine_ref, other_ref, total_ref, dk_ref, *refs):
    odd, small_refs, (wi_ref, bi_ref, wo_ref, w_ref) = lax.rem(me_ref[0], 2), refs[:5], refs[5:]
    total = total_ref[...] * scale
    units = wi_ref.shape[0]
    high = (total.shape[0] - 16) // 3
    rest = total[high : high + units]
    wi_ref[:, 0:LANE] = total[0:units]
    wi_ref[:, LANE : LANE + 64] = rest[:, 0:64]
    wo_ref[:, 0:LANE] = total[2 * high : 2 * high + units]
    wo_ref[:, LANE : LANE + 64] = rest[:, 64:LANE]
    bi_ref[...] = total[3 * high : 3 * high + 1, 0:units]
    w_ref[odd] = mine_ref[...].astype(F32) * scale
    w_ref[1 - odd] = other_ref[...].astype(F32) * scale
    for g in range(49):
        half, row = main_at(g)
        dk_ref[g // 7, g % 7, :, 0:LANE] = w_ref[half, row : row + 7]
        row, lane = rest_at(g)
        dk_ref[g // 7, g % 7, :, LANE : LANE + 64] = w_ref[1, row : row + 7][:, lane : lane + 64]
    for i, ref in enumerate(small_refs):
        ref[:, 0:LANE] = w_ref[0, 266 + i : 267 + i]
        ref[:, LANE : LANE + 64] = w_ref[1, 252 + i : 253 + i, 0:64]


def back_kernel(last, me_ref, g_ref, p_ref, q_ref, t_ref, c_ref, xf_ref, branch_ref, dx_ref, out_ref, z_ref, s_ref, u_ref):
    fill_rim(last, me_ref, p_ref, q_ref, z_ref)
    for i in range(4):
        split(g_ref[i].astype(F32), z_ref, 3 + i)
    out_ref[...] = (xf_ref[...] + branch_ref[...]).reshape(out_ref.shape).astype(BF16)
    stencil(z_ref, t_ref, s_ref, u_ref, True)
    main, rest = from_points(4, lambda u: u_ref[u], 6)
    for i in range(4):
        cot = c_ref[64 * i : 64 * i + 64].reshape(8, 8, c_ref.shape[1])
        dx_ref[i, :, :, 0:LANE] = (cot[:, :, 0:LANE] + main[i]).astype(BF16)
        dx_ref[i, :, :, LANE : LANE + 64] = (cot[:, :, LANE:] + rest[i][:, :, 0:64]).astype(BF16)


def params(mib):
    return pltpu.CompilerParams(vmem_limit_bytes=mib * 1024 * 1024)


def cost(us):
    return pl.CostEstimate(flops=int(us * 1.0e9), bytes_accessed=0, transcendentals=0)


def struct(shape, dtype):
    return jax.ShapeDtypeStruct(shape, dtype)


def on_device(
    features, cotangent, kernel, b_dw, ln_gain, ln_bias, w_in_t, b_in, w_out, b_out, gamma
):
    size_x, size_y, size_z, chans = features.shape
    devices = lax.axis_size("space")
    scale = float(size_x * devices * size_y * size_z) ** (-0.5)
    rows = size_x * size_y * size_z
    units = w_in_t.shape[0]
    bits = [1 << i for i in range(devices.bit_length() - 1)]
    order, sums_order = bits, [bits[0], bits[-1], bits[1]] + bits[2:-1]
    me = lax.axis_index("space").astype(jnp.int32).reshape(1)
    def call(body, name, us, mib, out_shape, operands, scratch=(), spec=VMEM):
        specs = [SMEM if x is me else spec for x in operands]
        return pl.pallas_call(
            body,
            out_shape=out_shape,
            in_specs=specs,
            out_specs=jax.tree.map(lambda _: VMEM, out_shape),
            scratch_shapes=list(scratch),
            compiler_params=params(mib),
            name=name,
            cost_estimate=cost(us),
        )(*operands)

    z_scratch = pltpu.VMEM((2, 10, size_y, size_z, LANE), F32)
    u_scratch = pltpu.VMEM((15, size_y, size_z, LANE), F32)
    shifts = (7, 15, size_y, size_z, LANE)
    cells = struct((rows, chans), F32)

    high = -(-units // 16) * 16
    lines = 3 * high + 16
    rim = struct((3 * size_y * size_z * 3 // 2, LANE), BF16)
    raw = (w_in_t, b_in, w_out, features)
    piece, to_core, to_far = call(
        pack_kernel,
        "pack",
        1.0,
        56,
        (struct((lines, LANE), BF16), rim, rim),
        (me,) + raw,
        [pltpu.VMEM(x.shape, x.dtype) for x in raw] + [pltpu.SemaphoreType.DMA((4,))],
        HBM,
    )
    x_core, x_far = swap(to_core, 1), swap_odd(to_far)
    weights = swap(piece, order[-1])
    given = (features, cotangent, kernel, b_dw, ln_gain, ln_bias, b_out, gamma, piece)
    prepared = call(
        prepare_kernel,
        "prepare",
        1.0,
        6,
        (
            struct((lines, LANE), BF16),
            struct((2, 4, size_y, size_z, LANE), F32),
            struct((16, 7, 8, LANE), F32),
            struct((8, chans), F32),
            cells,
            cells,
            struct((rows, 256), BF16),
        ),
        given,
        [pltpu.VMEM((2, 7, 7, 8, LANE), F32)]
        + [pltpu.VMEM(x.shape, x.dtype) for x in given[:-1]]
        + [pltpu.SemaphoreType.DMA((len(given),))],
        HBM,
    )
    weights, prepared = lax.optimization_barrier((weights, prepared))
    piece, own, taps, vecs, x_f32, cot_f32, d_branch = prepared
    weights = jnp.stack([piece, weights])
    for bit in order[-2:2:-1]:
        weights = jnp.concatenate([weights, swap(weights, bit)], axis=0)
    over_z, over_x = swap(weights, order[2]), swap(weights, order[1])
    over_z, over_x, x_far, x_core = lax.optimization_barrier((over_z, over_x, x_far, x_core))
    weights = jnp.concatenate([weights, over_z, over_x, swap(over_z, order[1])], axis=0)
    forward = call(
        functools.partial(forward_kernel, devices - 1),
        "forward_stencil",
        2.5,
        10,
        (struct((rows, 256), BF16), struct((rows, 256), F32), struct(shifts, F32)),
        (me, own, x_core, x_far, taps, vecs),
        [z_scratch, u_scratch, pltpu.VMEM((rows, chans), F32)],
    )
    weights, forward = lax.optimization_barrier((weights, forward))
    normed, unit, shifted_x = forward
    weights_other = swap(weights, 1)

    pieces = weights.shape[0]
    branch, d_mixed, to_far, grad_keep, to_core, small = call(
        pointwise_kernel,
        "pointwise",
        2.5,
        16,
        (
            cells,
            struct(features.shape, BF16),
            rim,
            struct((pieces * lines, LANE), F32),
            struct((pieces * lines + rim.shape[0], LANE), BF16),
            struct((8, 256), F32),
        ),
        (me, weights, weights_other, normed, unit, x_f32, cot_f32, d_branch, vecs),
        [pltpu.VMEM((2 * pieces * high, 256), BF16)] * 2
        + [pltpu.VMEM((2 * pieces * high, 256), F32)] * 2
        + [pltpu.VMEM((size_x, size_y * size_z, chans), F32)],
    )
    keep, send = call(
        grad_kernel,
        "kernel_gradient",
        2.0,
        10,
        (struct((HALF, LANE), F32), struct((HALF, LANE), BF16)),
        (me, shifted_x, d_mixed, small),
        [
            pltpu.VMEM((2, 4, size_y, size_z, LANE), F32),
            u_scratch,
            pltpu.VMEM((15, 7, 8, LANE), F32),
            pltpu.VMEM((448, LANE), F32),
            pltpu.VMEM((448, LANE), F32),
            pltpu.VMEM((2, HALF, LANE), F32),
            pltpu.VMEM((7, 64, LANE), F32),
        ],
    )

    from_core = swap(to_core, 1)
    total = grad_keep + from_core[: pieces * lines].astype(F32)
    g_core = from_core[pieces * lines :]
    sums = keep + swap(send, 1).astype(F32)
    sums, to_far = lax.optimization_barrier((sums, to_far))
    g_far = swap_odd(to_far)
    for step, (bit, sums_bit) in enumerate(zip(order[1:], sums_order[1:])):
        n = total.shape[0] // 2
        mine, kept = sums.astype(BF16), total[:n]
        theirs = swap(mine, sums_bit)
        got = swap(total[n:].astype(BF16), bit)
        if step == len(order) - 3:
            d_x, output = call(
                functools.partial(back_kernel, devices - 1),
                "backward_stencil",
                2.5,
                10,
                (struct(features.shape, BF16),) * 2,
                (me, d_mixed, g_core, g_far, taps, cot_f32, x_f32, branch),
                [z_scratch, pltpu.VMEM(shifts, F32), u_scratch],
            )
            theirs, d_x, output = lax.optimization_barrier((theirs, d_x, output))
        if step < len(order) - 2:
            theirs, got = lax.optimization_barrier((theirs, got))
        sums = mine.astype(F32) + theirs.astype(F32)
        total = kept + got.astype(F32)
    mine = sums.astype(BF16)
    other = swap(mine, 1)
    total = lax.optimization_barrier(kept + got.astype(F32))
    d_kernel, *vectors, d_w_in, d_b_in, d_w_out = call(
        functools.partial(final_kernel, scale),
        "final",
        1.0,
        4,
        (struct(kernel.shape, F32),)
        + (struct((1, chans), F32),) * 5
        + (struct((units, chans), F32), struct((1, units), F32), struct((units, chans), F32)),
        (me, mine, other, total),
        [pltpu.VMEM((2, HALF, LANE), F32)],
    )
    d_b_dw, d_ln_gain, d_ln_bias, d_b_out, d_gamma = [v.reshape(chans) for v in vectors]
    return (
        output,
        d_x,
        d_kernel,
        d_b_dw,
        d_ln_gain,
        d_ln_bias,
        d_w_in,
        d_b_in.reshape(units),
        d_w_out,
        d_b_out,
        d_gamma,
    )


def solution(mesh):
    in_specs = (
        P(("crop", "space"), None, None, None),
        P(("crop", "space"), None, None, None),
        P(),
        P(),
        P(),
        P(),
        P("space", None),
        P("space"),
        P("space", None),
        P(),
        P(),
    )
    out_specs = (
        P(("crop", "space"), None, None, None),
        P(("crop", "space"), None, None, None),
        P("crop", None, None, None),
        P("crop"),
        P("crop"),
        P("crop"),
        P(("crop", "space"), None),
        P(("crop", "space")),
        P(("crop", "space"), None),
        P("crop"),
        P("crop"),
    )
    return jax.shard_map(
        on_device, mesh=mesh, in_specs=in_specs, out_specs=out_specs, check_vma=False
    )
```

```python
import functools

import jax
import jax.numpy as jnp
import numpy as np
from jax import lax
from jax.experimental import pallas as pl
from jax.experimental.pallas import tpu as pltpu
from jax.sharding import PartitionSpec as P

root_half = 0.7071067811865476
inv_root_tau = 0.3989422804014327
F32 = jnp.float32
BF16 = jnp.bfloat16
LANE = 128
VMEM = pl.BlockSpec(memory_space=pltpu.VMEM)
HBM = pl.BlockSpec(memory_space=pltpu.HBM)
SMEM = pl.BlockSpec(memory_space=pltpu.SMEM)

POINTS = (0.4, 0.8, 1.25, 2.5)
PAIRS = len(POINTS)


def analysis():
    finite = [0.0] + [sign * p for p in POINTS for sign in (1.0, -1.0)]
    vander = np.array([[x**k for k in range(10)] for x in finite] + [[0.0] * 9 + [1.0]])
    inverse = np.linalg.inv(vander).T
    even = [{k: float(inverse[1 + 2 * q, k]) for k in (2, 4, 6, 8)} for q in range(PAIRS)]
    odd = [{k: float(inverse[1 + 2 * q, k]) for k in (1, 3, 5, 7)} for q in range(PAIRS)]
    zero = {k: float(inverse[0, k]) for k in (0, 2, 4, 6, 8)}
    infinity = {k: float(inverse[9, k]) for k in (1, 3, 5, 7, 9)}
    return even, odd, zero, infinity


def evaluation(size):
    even = [{k: p**k for k in range(0, size, 2)} for p in POINTS]
    odd = [{k: p**k for k in range(1, size, 2)} for p in POINTS]
    return even, odd, {0: 1.0}, {size - 1: 1.0}


def weighted(load, weights):
    total = None
    for k, w in weights.items():
        term = load(k) if w == 1.0 else load(k) * w
        total = term if total is None else total + term
    return total


def low_lanes(shape):
    return lax.broadcasted_iota(jnp.int32, shape, len(shape) - 1) < 64


def to_points(tables, main, rest, store):
    even, odd, zero, infinity = tables
    for q in range(PAIRS):
        e, o = weighted(main, even[q]), weighted(main, odd[q])
        store(1 + 2 * q, e + o)
        store(2 + 2 * q, e - o)
        e, o = weighted(rest, even[q]), weighted(rest, odd[q])
        store(10 + q, jnp.where(low_lanes(e.shape), e + o, e - o))
    store(0, weighted(main, zero))
    store(9, weighted(main, infinity))
    z, i = weighted(rest, zero), weighted(rest, infinity)
    store(14, jnp.where(low_lanes(z.shape), z, i))


def from_points(size, load, power=0):
    main, rest = [None] * size, [None] * size

    def add(into, k, v, w):
        term = v if w == 1.0 else v * w
        into[k] = term if into[k] is None else into[k] + term

    for q in range(PAIRS):
        plus, minus, both = load(1 + 2 * q), load(2 + 2 * q), load(10 + q)
        swapped = pltpu.roll(both, 64, axis=both.ndim - 1)
        sums = (plus + minus, both + swapped), (plus - minus, both - swapped)
        for k in range(size):
            m, r = sums[k % 2]
            add(main, k, m, POINTS[q] ** (k + power))
            add(rest, k, r, POINTS[q] ** (k + power))
    ends = load(14)
    add(main, 0, load(0), 1.0)
    add(rest, 0, ends, 1.0)
    add(main, size - 1, load(9), 1.0)
    add(rest, size - 1, pltpu.roll(ends, 64, axis=ends.ndim - 1), 1.0)
    return main, rest


def swap(x, bit):
    size = lax.axis_size("space")
    return lax.ppermute(x, "space", [(i, i ^ bit) for i in range(size)])


def swap_odd(x):
    size = lax.axis_size("space")
    return lax.ppermute(x, "space", [(i, (i + 1 if i % 2 else i - 1) % size) for i in range(size)])


def shifted(v, by):
    if by == 0:
        return v
    row = lax.broadcasted_iota(jnp.int32, v.shape, 0)
    keep = (row < 8 - by) if by > 0 else (row >= -by)
    return jnp.where(keep, pltpu.roll(v, (-by) % 8, axis=0), 0.0)


def split(v, z_ref, plane):
    z_ref[0, plane] = v[..., :LANE]
    z_ref[1, plane, ..., 0:64] = v[..., LANE:]
    z_ref[1, plane, ..., 64:128] = v[..., LANE:]


def pack_planes(first, load, out_ref, base=0):
    for k in range(3):
        v = load(first + k)
        cells = v.shape[0]
        at = base + k * cells * 3 // 2
        out_ref[at : at + cells] = v[:, :LANE].astype(BF16)
        pair = jnp.concatenate([v[: cells // 2, LANE:], v[cells // 2 :, LANE:]], axis=1)
        out_ref[at + cells : at + cells * 3 // 2] = pair.astype(BF16)


def fill_rim(last, me_ref, p_ref, q_ref, z_ref):
    me = me_ref[0]
    odd = lax.rem(me, 2) == 1
    p, q = p_ref[...].astype(F32), q_ref[...].astype(F32)
    before = jnp.where(me == 0, 0.0, jnp.where(odd, p, q))
    after = jnp.where(me == last, 0.0, jnp.where(odd, q, p))
    rows, cols = z_ref.shape[2], z_ref.shape[3]
    cells = rows * cols
    for k in range(3):
        at = k * cells * 3 // 2
        for v, plane in ((before, k), (after, k + 7)):
            z_ref[0, plane] = v[at : at + cells].reshape(rows, cols, LANE)
            pair = v[at + cells : at + cells * 3 // 2]
            swapped = pltpu.roll(pair, 64, axis=1)
            low = low_lanes(pair.shape)
            z_ref[1, plane, : rows // 2] = jnp.where(low, pair, swapped).reshape(rows // 2, cols, LANE)
            z_ref[1, plane, rows // 2 :] = jnp.where(low, swapped, pair).reshape(rows // 2, cols, LANE)


def fill_taps(k_ref, r_ref, t_ref):
    for a in range(7):
        for b in range(7):
            v = k_ref[a, b]
            r_ref[0, a, b, 0:7] = v[:, :LANE]
            r_ref[1, a, b, 0:7, 0:64] = v[:, LANE:]
            r_ref[1, a, b, 0:7, 64:128] = v[:, LANE:]
    for b in range(7):

        def store(u, v):
            t_ref[u, b] = v
            if u == 14:
                t_ref[15, b] = pltpu.roll(v, 64, axis=1)

        to_points(evaluation(7), lambda k: r_ref[0, k, b], lambda k: r_ref[1, k, b], store)


def reversed_unit(u):
    same_sign = 2 * PAIRS - 1 - 2 * ((u - 1) // 2) + (u - 1) % 2
    paired = 19 + PAIRS - u
    return jnp.where(
        u == 0, 9, jnp.where(u < 9, same_sign, jnp.where(u == 9, 0, jnp.where(u < 14, paired, 15)))
    )


def stencil(z_ref, t_ref, s_ref, u_ref, flip):
    def row(j, carry):
        def store(u, v):
            s_ref[3, u, j] = v

        to_points(analysis(), lambda k: z_ref[0, k, j], lambda k: z_ref[1, k, j], store)
        return carry

    lax.fori_loop(0, 8, row, 0, unroll=8)

    def unit(u, carry):
        taps_at = reversed_unit(u) if flip else u
        rows = [s_ref[3, u, j] for j in range(8)]
        for e in range(7):
            if e != 3:
                for j in range(8):
                    s_ref[e, u, j] = shifted(rows[j], e - 3)
        acc = [None] * 8
        for e in range(7):
            taps = []
            for b in range(7):
                fb, fe = (6 - b, 6 - e) if flip else (b, e)
                taps.append(jnp.broadcast_to(t_ref[taps_at, fb, fe : fe + 1], (8, LANE)))
            for source in range(8):
                x = rows[source] if e == 3 else s_ref[e, u, source]
                for b in range(7):
                    j = source - b + 3
                    if 0 <= j < 8:
                        term = x * taps[b]
                        acc[j] = term if acc[j] is None else acc[j] + term
        for j in range(8):
            u_ref[u, j] = acc[j]
        return carry

    lax.fori_loop(0, 3 * (PAIRS + 1), unit, 0, unroll=3)


def fetch(sources, targets, sem):
    copies = [pltpu.make_async_copy(x, y, sem.at[i]) for i, (x, y) in enumerate(zip(sources, targets))]
    for copy in copies:
        copy.start()
    return copies


def pack_kernel(me_ref, wi_hbm, b_hbm, wo_hbm, x_hbm, out_ref, core_ref, far_ref, wi_ref, b_ref, wo_ref, x_ref, sem):
    copies = fetch((x_hbm, wi_hbm, b_hbm, wo_hbm), (x_ref, wi_ref, b_ref, wo_ref), sem)
    units = wi_ref.shape[0]
    high = (out_ref.shape[0] - 16) // 3
    out_ref[...] = jnp.zeros(out_ref.shape, BF16)
    for copy in copies:
        copy.wait()
    w_in, w_out = wi_ref[...].astype(F32), wo_ref[...].astype(F32)
    out_ref[0:units] = w_in[:, :LANE].astype(BF16)
    out_ref[high : high + units] = jnp.concatenate([w_in[:, LANE:], w_out[:, LANE:]], axis=1).astype(BF16)
    out_ref[2 * high : 2 * high + units] = w_out[:, :LANE].astype(BF16)
    line = b_ref[...].astype(F32).reshape(1, units)
    line = jnp.concatenate([line, jnp.zeros((1, LANE - units), F32)], axis=1)
    first = lax.broadcasted_iota(jnp.int32, (16, LANE), 0) == 0
    out_ref[3 * high : 3 * high + 16] = jnp.where(first, jnp.broadcast_to(line, (16, LANE)), 0.0).astype(BF16)
    odd = lax.rem(me_ref[0], 2)

    def plane(i):
        v = x_ref[i].astype(F32)
        return v.reshape(v.shape[0] * v.shape[1], v.shape[2])

    pack_planes(1 - odd, plane, core_ref)
    pack_planes(odd, plane, far_ref)


def gather_lines(lines, high):
    count = -(-len(lines) * high // LANE)
    out = [jnp.zeros((8, LANE), F32)] * count
    lane = lax.broadcasted_iota(jnp.int32, (8, LANE), 1)
    for i, line in enumerate(lines):
        at, shift = divmod(i * high, LANE)
        moved = pltpu.roll(line, shift, axis=1) if shift else line
        out[at] = out[at] + jnp.where(lane >= shift, moved, 0.0)
        if shift + high > LANE:
            out[at + 1] = out[at + 1] + jnp.where(lane < shift, moved, 0.0)
    return out


def scatter_lines(full, count, high):
    lane = lax.broadcasted_iota(jnp.int32, (8, LANE), 1)
    lines = []
    for i in range(count):
        at, shift = divmod(i * high, LANE)
        v = pltpu.roll(full[at], LANE - shift, axis=1) if shift else full[at]
        if shift + high > LANE:
            v = jnp.where(lane < LANE - shift, v, pltpu.roll(full[at + 1], LANE - shift, axis=1))
        lines.append(jnp.where(lane < high, v, 0.0))
    return lines


def prepare_kernel(*refs):
    sources, refs = refs[:9], refs[9:]
    (w_ref, z_ref, t_ref, vec_ref, xf_ref, cf_ref, db_ref), refs = refs[:7], refs[7:]
    r_ref, x_ref, c_ref, k_ref, *vec_refs, sem = refs
    copies = fetch(sources, (x_ref, c_ref, k_ref, *vec_refs, w_ref), sem)
    copies[2].wait()
    fill_taps(k_ref, r_ref, t_ref)
    for copy in copies[:2] + copies[3:]:
        copy.wait()
    rows, chans = xf_ref.shape
    for i, ref in enumerate(vec_refs):
        vec_ref[i : i + 1] = ref[...].reshape(1, chans)
    for i in range(4):
        split(x_ref[i].astype(F32), z_ref, i)
    xf_ref[...] = x_ref[...].astype(F32).reshape(rows, chans)
    cot = c_ref[...].astype(F32).reshape(rows, chans)
    cf_ref[...] = cot
    d_branch = cot * vec_ref[4:5]
    vec_ref[5:6] = jnp.sum(d_branch, axis=0, keepdims=True)
    vec_ref[6:8] = jnp.zeros((2, chans), F32)
    db_ref[...] = jnp.concatenate([d_branch, jnp.zeros((rows, 256 - chans), F32)], axis=1).astype(BF16)


def forward_kernel(last, me_ref, own_ref, p_ref, q_ref, t_ref, vec_ref, na_ref, unit_ref, s_ref, z_ref, u_ref, m_ref):
    fill_rim(last, me_ref, p_ref, q_ref, z_ref)
    z_ref[:, 3:7] = own_ref[...]
    stencil(z_ref, t_ref, s_ref, u_ref, False)

    def row(j, carry):
        main, rest = from_points(4, lambda u: u_ref[u, j])
        for i in range(4):
            at = pl.ds(pl.multiple_of(64 * i + 8 * j, 8), 8)
            m_ref[at, 0:LANE] = main[i]
            m_ref[at, LANE : LANE + 64] = rest[i][:, 0:64]
        return carry

    lax.fori_loop(0, 8, row, 0, unroll=8)
    chans = m_ref.shape[1]
    mixed = m_ref[...] + vec_ref[0:1]
    centred = mixed - jnp.mean(mixed, axis=-1, keepdims=True)
    inverse = lax.rsqrt(jnp.mean(centred * centred, axis=-1, keepdims=True) + 1e-06)
    unit = centred * inverse
    normed = unit * vec_ref[1:2] + vec_ref[2:3]
    rows = unit.shape[0]
    na_ref[:, 0:chans] = normed.astype(BF16)
    na_ref[:, chans:256] = jnp.zeros((rows, 256 - chans), BF16)
    unit_ref[:, 0:chans] = unit
    unit_ref[:, chans:256] = jnp.broadcast_to(inverse, (rows, 256 - chans))


def pointwise_kernel(me_ref, g0_ref, g1_ref, na_ref, unit_ref, xf_ref, cf_ref, db_ref, vec_ref, branch_ref, dm_ref, far_ref, w0_ref, w1_ref, small_ref, wi_ref, wo_ref, di_ref, do_ref, m_ref):
    rows, chans = xf_ref.shape
    normed = na_ref[...]
    d_b = db_ref[...]
    gamma = vec_ref[4:5]
    branch = jnp.zeros((rows, 256), F32)
    d_normed = jnp.zeros((rows, 256), F32)
    over_c = (((1,), (1,)), ((), ()))
    over_rows = (((0,), (0,)), ((), ()))
    pieces, high = g0_ref.shape[0], (g0_ref.shape[1] - 16) // 3
    low = low_lanes((high, LANE))
    first_row = lax.broadcasted_iota(jnp.int32, (16, LANE), 0) == 0
    lines, d_bias = [], []
    for i in range(2 * pieces):
        here = slice(i * high, i * high + high)
        g_ref, k = (g0_ref, i) if i < pieces else (g1_ref, i - pieces)
        rest = g_ref[k, high : 2 * high].astype(F32)
        wi_ref[here, 0:LANE] = g_ref[k, 0:high]
        wi_ref[here, LANE:256] = jnp.where(low, rest, 0.0).astype(BF16)
        wo_ref[here, 0:LANE] = g_ref[k, 2 * high : 3 * high]
        wo_ref[here, LANE:256] = jnp.where(low, pltpu.roll(rest, 64, axis=1), 0.0).astype(BF16)
        line = g_ref[k, 3 * high : 3 * high + 16].astype(F32)[0:1]
        lines.append(jnp.broadcast_to(line, (8, LANE)))
    bias = gather_lines(lines, high)
    total = 2 * pieces * high
    step = next(n for n in (768, 512, 256) if total % n == 0)
    for first in range(0, total, step):
        here = slice(first, first + step)
        w_in, w_out = wi_ref[here], wo_ref[here]
        line = jnp.concatenate([v[0:1] for v in bias[first // LANE : (first + step) // LANE]], axis=1)
        pre = lax.dot_general(normed, w_in, over_c, preferred_element_type=F32) + line
        d_hidden = lax.dot_general(d_b, w_out, over_c, preferred_element_type=F32)
        cdf = 0.5 * (1.0 + lax.erf(pre * root_half))
        hidden = (pre * cdf).astype(BF16)
        slope = cdf + pre * jnp.exp(-0.5 * pre * pre) * inv_root_tau
        d_pre = d_hidden * slope
        line = jnp.sum(d_pre, axis=0, keepdims=True)
        for at in range(0, step, LANE):
            d_bias.append(jnp.broadcast_to(line[:, at : at + LANE], (8, LANE)))
        d_pre = d_pre.astype(BF16)
        branch = branch + jnp.dot(hidden, w_out, preferred_element_type=F32)
        d_normed = d_normed + jnp.dot(d_pre, w_in, preferred_element_type=F32)
        di_ref[here] = lax.dot_general(d_pre, normed, over_rows, preferred_element_type=F32)
        do_ref[here] = lax.dot_general(hidden, d_b, over_rows, preferred_element_type=F32)
    for i, line in enumerate(scatter_lines(d_bias, 2 * pieces, high)):
        here = slice(i * high, i * high + high)
        w_ref, k = (w0_ref, i) if i < pieces else (w1_ref, i - pieces)
        rest = jnp.where(low, di_ref[here, LANE:256], pltpu.roll(do_ref[here, LANE:256], 64, axis=1))
        at = k * (3 * high + 16)
        w_ref[at : at + high] = di_ref[here, 0:LANE].astype(w_ref.dtype)
        w_ref[at + high : at + 2 * high] = rest.astype(w_ref.dtype)
        w_ref[at + 2 * high : at + 3 * high] = do_ref[here, 0:LANE].astype(w_ref.dtype)
        line = jnp.where(first_row, jnp.broadcast_to(line[0:1], (16, LANE)), 0.0)
        w_ref[at + 3 * high : at + 3 * high + 16] = line.astype(w_ref.dtype)
    branch = branch[:, 0:chans] + vec_ref[3:4]
    branch_ref[...] = gamma * branch
    d_normed = d_normed[:, 0:chans]
    unit = unit_ref[:, 0:chans]
    inverse = unit_ref[:, chans : chans + 1]
    scaled = d_normed * vec_ref[1:2]
    d_mixed = inverse * (
        scaled
        - jnp.mean(scaled, axis=-1, keepdims=True)
        - unit * jnp.mean(scaled * unit, axis=-1, keepdims=True)
    )
    dm_ref[...] = d_mixed.reshape(dm_ref.shape).astype(BF16)
    m_ref[...] = d_mixed.reshape(m_ref.shape)
    odd = lax.rem(me_ref[0], 2)
    pack_planes(1 - odd, lambda i: m_ref[i], w1_ref, w0_ref.shape[0])
    pack_planes(odd, lambda i: m_ref[i], far_ref)
    small_ref[...] = jnp.zeros(small_ref.shape, F32)
    sums = (d_mixed, d_normed * unit, d_normed, None, cf_ref[...] * branch)
    for i, term in enumerate(sums):
        total = vec_ref[5:6] if term is None else jnp.sum(term, axis=0, keepdims=True)
        small_ref[i : i + 1, 0:chans] = total


def rows_to_one(v, p_ref):
    for b, x in enumerate(v):
        p_ref[8 * b : 8 * b + 8] = x
    total = p_ref[pl.ds(0, 8, stride=8), :]
    for k in range(1, 8):
        total = total + p_ref[pl.ds(k, 8, stride=8), :]
    return total


HALF = 272


def block(g):
    return 64 * (g // 7) + 8 * (g % 7)


def main_at(g):
    return (0, 7 * g) if g < 38 else (1, 7 * (g - 38))


def rest_at(g):
    return 77 + 7 * (g % 25), 64 * (g // 25)


def grad_kernel(me_ref, s_ref, g_ref, small_ref, keep_ref, send_ref, z_ref, t_ref, o_ref, wa_ref, wb_ref, w_ref, p_ref):
    p_ref[:, 56:64] = jnp.zeros((7, 8, LANE), F32)
    odd = lax.rem(me_ref[0], 2)
    for i in range(4):
        split(g_ref[i].astype(F32), z_ref, i)

    def row(j, carry):
        def store(u, v):
            t_ref[u, j] = v

        to_points(evaluation(4), lambda k: z_ref[0, k, j], lambda k: z_ref[1, k, j], store)
        return carry

    lax.fori_loop(0, 8, row, 0, unroll=8)

    def unit(u, carry):
        grads = [t_ref[u, j] for j in range(8)]
        for e in range(7):
            acc = [None] * 7
            for source in range(8):
                x = s_ref[e, u, source]
                for b in range(7):
                    j = source - b + 3
                    if 0 <= j < 8:
                        term = x * grads[j]
                        acc[b] = term if acc[b] is None else acc[b] + term
            o_ref[u, e] = rows_to_one(acc, p_ref.at[e])
        return carry

    lax.fori_loop(0, 3 * (PAIRS + 1), unit, 0, unroll=3)

    for e in range(7):
        main, rest = from_points(7, lambda u: o_ref[u, e])
        for a in range(7):
            wa_ref[pl.ds(a * 64 + e, 8, stride=8), :] = main[a]
            one = jnp.where(low_lanes((8, LANE)), rest[a], pltpu.roll(rest[a], 64, axis=1))
            wb_ref[pl.ds(a * 64 + e, 8, stride=8), :] = one

    w_ref[0, HALF - 16 : HALF] = jnp.zeros((16, LANE), F32)
    w_ref[1, HALF - 16 : HALF] = jnp.zeros((16, LANE), F32)
    low = low_lanes((8, LANE))[0:7]
    for g in range(49):
        half, row = main_at(g)
        w_ref[half, row : row + 7] = wa_ref[block(g) : block(g) + 7]
        row, lane = rest_at(g)
        if lane == 0:
            pair = min(g + 25, 48)
            w_ref[1, row : row + 7] = jnp.where(
                low, wb_ref[block(g) : block(g) + 7], wb_ref[block(pair) : block(pair) + 7]
            )
    w_ref[0, 266:271] = small_ref[0:5, 0:LANE]
    w_ref[1, 252:257] = small_ref[0:5, LANE:256]
    keep_ref[...] = w_ref[odd]
    send_ref[...] = w_ref[1 - odd].astype(BF16)


def final_kernel(scale, me_ref, mine_ref, other_ref, total_ref, dk_ref, *refs):
    odd, small_refs, (wi_ref, bi_ref, wo_ref, w_ref) = lax.rem(me_ref[0], 2), refs[:5], refs[5:]
    total = total_ref[...] * scale
    units = wi_ref.shape[0]
    high = (total.shape[0] - 16) // 3
    rest = total[high : high + units]
    wi_ref[:, 0:LANE] = total[0:units]
    wi_ref[:, LANE : LANE + 64] = rest[:, 0:64]
    wo_ref[:, 0:LANE] = total[2 * high : 2 * high + units]
    wo_ref[:, LANE : LANE + 64] = rest[:, 64:LANE]
    bi_ref[...] = total[3 * high : 3 * high + 1, 0:units]
    w_ref[odd] = mine_ref[...].astype(F32) * scale
    w_ref[1 - odd] = other_ref[...].astype(F32) * scale
    for g in range(49):
        half, row = main_at(g)
        dk_ref[g // 7, g % 7, :, 0:LANE] = w_ref[half, row : row + 7]
        row, lane = rest_at(g)
        dk_ref[g // 7, g % 7, :, LANE : LANE + 64] = w_ref[1, row : row + 7][:, lane : lane + 64]
    for i, ref in enumerate(small_refs):
        ref[:, 0:LANE] = w_ref[0, 266 + i : 267 + i]
        ref[:, LANE : LANE + 64] = w_ref[1, 252 + i : 253 + i, 0:64]


def back_kernel(last, me_ref, g_ref, p_ref, q_ref, t_ref, c_ref, xf_ref, branch_ref, dx_ref, out_ref, z_ref, s_ref, u_ref):
    fill_rim(last, me_ref, p_ref, q_ref, z_ref)
    for i in range(4):
        split(g_ref[i].astype(F32), z_ref, 3 + i)
    out_ref[...] = (xf_ref[...] + branch_ref[...]).reshape(out_ref.shape).astype(BF16)
    stencil(z_ref, t_ref, s_ref, u_ref, True)
    main, rest = from_points(4, lambda u: u_ref[u], 6)
    for i in range(4):
        cot = c_ref[64 * i : 64 * i + 64].reshape(8, 8, c_ref.shape[1])
        dx_ref[i, :, :, 0:LANE] = (cot[:, :, 0:LANE] + main[i]).astype(BF16)
        dx_ref[i, :, :, LANE : LANE + 64] = (cot[:, :, LANE:] + rest[i][:, :, 0:64]).astype(BF16)


def params(mib):
    return pltpu.CompilerParams(vmem_limit_bytes=mib * 1024 * 1024)


def cost(us):
    return pl.CostEstimate(flops=int(us * 1.0e9), bytes_accessed=0, transcendentals=0)


def struct(shape, dtype):
    return jax.ShapeDtypeStruct(shape, dtype)


def on_device(
    features, cotangent, kernel, b_dw, ln_gain, ln_bias, w_in_t, b_in, w_out, b_out, gamma
):
    size_x, size_y, size_z, chans = features.shape
    devices = lax.axis_size("space")
    scale = float(size_x * devices * size_y * size_z) ** (-0.5)
    rows = size_x * size_y * size_z
    units = w_in_t.shape[0]
    bits = [1 << i for i in range(devices.bit_length() - 1)]
    order, sums_order = bits, [bits[0], bits[-1], bits[1]] + bits[2:-1]
    me = lax.axis_index("space").astype(jnp.int32).reshape(1)
    def call(body, name, us, mib, out_shape, operands, scratch=(), spec=VMEM):
        specs = [SMEM if x is me else spec for x in operands]
        return pl.pallas_call(
            body,
            out_shape=out_shape,
            in_specs=specs,
            out_specs=jax.tree.map(lambda _: VMEM, out_shape),
            scratch_shapes=list(scratch),
            compiler_params=params(mib),
            name=name,
            cost_estimate=cost(us),
        )(*operands)

    z_scratch = pltpu.VMEM((2, 10, size_y, size_z, LANE), F32)
    u_scratch = pltpu.VMEM((15, size_y, size_z, LANE), F32)
    shifts = (7, 15, size_y, size_z, LANE)
    cells = struct((rows, chans), F32)

    high = -(-units // 16) * 16
    lines = 3 * high + 16
    rim = struct((3 * size_y * size_z * 3 // 2, LANE), BF16)
    raw = (w_in_t, b_in, w_out, features)
    piece, to_core, to_far = call(
        pack_kernel,
        "pack",
        1.0,
        56,
        (struct((lines, LANE), BF16), rim, rim),
        (me,) + raw,
        [pltpu.VMEM(x.shape, x.dtype) for x in raw] + [pltpu.SemaphoreType.DMA((4,))],
        HBM,
    )
    x_core, x_far = swap(to_core, 1), swap_odd(to_far)
    weights = swap(piece, order[-1])
    given = (features, cotangent, kernel, b_dw, ln_gain, ln_bias, b_out, gamma, piece)
    prepared = call(
        prepare_kernel,
        "prepare",
        1.0,
        6,
        (
            struct((lines, LANE), BF16),
            struct((2, 4, size_y, size_z, LANE), F32),
            struct((16, 7, 8, LANE), F32),
            struct((8, chans), F32),
            cells,
            cells,
            struct((rows, 256), BF16),
        ),
        given,
        [pltpu.VMEM((2, 7, 7, 8, LANE), F32)]
        + [pltpu.VMEM(x.shape, x.dtype) for x in given[:-1]]
        + [pltpu.SemaphoreType.DMA((len(given),))],
        HBM,
    )
    weights, prepared = lax.optimization_barrier((weights, prepared))
    piece, own, taps, vecs, x_f32, cot_f32, d_branch = prepared
    weights = jnp.stack([piece, weights])
    for bit in order[-2:2:-1]:
        weights = jnp.concatenate([weights, swap(weights, bit)], axis=0)
    over_z, over_x = swap(weights, order[2]), swap(weights, order[1])
    over_z, over_x, x_far, x_core = lax.optimization_barrier((over_z, over_x, x_far, x_core))
    weights = jnp.concatenate([weights, over_z, over_x, swap(over_z, order[1])], axis=0)
    forward = call(
        functools.partial(forward_kernel, devices - 1),
        "forward_stencil",
        2.5,
        10,
        (struct((rows, 256), BF16), struct((rows, 256), F32), struct(shifts, F32)),
        (me, own, x_core, x_far, taps, vecs),
        [z_scratch, u_scratch, pltpu.VMEM((rows, chans), F32)],
    )
    weights, forward = lax.optimization_barrier((weights, forward))
    normed, unit, shifted_x = forward
    weights_other = swap(weights, 1)

    pieces = weights.shape[0]
    branch, d_mixed, to_far, grad_keep, to_core, small = call(
        pointwise_kernel,
        "pointwise",
        2.5,
        16,
        (
            cells,
            struct(features.shape, BF16),
            rim,
            struct((pieces * lines, LANE), F32),
            struct((pieces * lines + rim.shape[0], LANE), BF16),
            struct((8, 256), F32),
        ),
        (me, weights, weights_other, normed, unit, x_f32, cot_f32, d_branch, vecs),
        [pltpu.VMEM((2 * pieces * high, 256), BF16)] * 2
        + [pltpu.VMEM((2 * pieces * high, 256), F32)] * 2
        + [pltpu.VMEM((size_x, size_y * size_z, chans), F32)],
    )
    keep, send = call(
        grad_kernel,
        "kernel_gradient",
        2.0,
        10,
        (struct((HALF, LANE), F32), struct((HALF, LANE), BF16)),
        (me, shifted_x, d_mixed, small),
        [
            pltpu.VMEM((2, 4, size_y, size_z, LANE), F32),
            u_scratch,
            pltpu.VMEM((15, 7, 8, LANE), F32),
            pltpu.VMEM((448, LANE), F32),
            pltpu.VMEM((448, LANE), F32),
            pltpu.VMEM((2, HALF, LANE), F32),
            pltpu.VMEM((7, 64, LANE), F32),
        ],
    )

    from_core = swap(to_core, 1)
    total = grad_keep + from_core[: pieces * lines].astype(F32)
    g_core = from_core[pieces * lines :]
    sums = keep + swap(send, 1).astype(F32)
    sums, to_far = lax.optimization_barrier((sums, to_far))
    g_far = swap_odd(to_far)
    for step, (bit, sums_bit) in enumerate(zip(order[1:], sums_order[1:])):
        n = total.shape[0] // 2
        mine, kept = sums.astype(BF16), total[:n]
        theirs = swap(mine, sums_bit)
        got = swap(total[n:].astype(BF16), bit)
        if step == len(order) - 3:
            d_x, output = call(
                functools.partial(back_kernel, devices - 1),
                "backward_stencil",
                2.5,
                10,
                (struct(features.shape, BF16),) * 2,
                (me, d_mixed, g_core, g_far, taps, cot_f32, x_f32, branch),
                [z_scratch, pltpu.VMEM(shifts, F32), u_scratch],
            )
        if step < len(order) - 2:
            theirs, got = lax.optimization_barrier((theirs, got))
        sums = mine.astype(F32) + theirs.astype(F32)
        total = kept + got.astype(F32)
    mine = sums.astype(BF16)
    mine, d_x, output = lax.optimization_barrier((mine, d_x, output))
    other = swap(mine, 1)
    total = lax.optimization_barrier(kept + got.astype(F32))
    d_kernel, *vectors, d_w_in, d_b_in, d_w_out = call(
        functools.partial(final_kernel, scale),
        "final",
        1.0,
        4,
        (struct(kernel.shape, F32),)
        + (struct((1, chans), F32),) * 5
        + (struct((units, chans), F32), struct((1, units), F32), struct((units, chans), F32)),
        (me, mine, other, total),
        [pltpu.VMEM((2, HALF, LANE), F32)],
    )
    d_b_dw, d_ln_gain, d_ln_bias, d_b_out, d_gamma = [v.reshape(chans) for v in vectors]
    return (
        output,
        d_x,
        d_kernel,
        d_b_dw,
        d_ln_gain,
        d_ln_bias,
        d_w_in,
        d_b_in.reshape(units),
        d_w_out,
        d_b_out,
        d_gamma,
    )


def solution(mesh):
    in_specs = (
        P(("crop", "space"), None, None, None),
        P(("crop", "space"), None, None, None),
        P(),
        P(),
        P(),
        P(),
        P("space", None),
        P("space"),
        P("space", None),
        P(),
        P(),
    )
    out_specs = (
        P(("crop", "space"), None, None, None),
        P(("crop", "space"), None, None, None),
        P("crop", None, None, None),
        P("crop"),
        P("crop"),
        P("crop"),
        P(("crop", "space"), None),
        P(("crop", "space")),
        P(("crop", "space"), None),
        P("crop"),
        P("crop"),
    )
    return jax.shard_map(
        on_device, mesh=mesh, in_specs=in_specs, out_specs=out_specs, check_vma=False
    )
```
